128 devices in a mesh: seq: 16 (over y, z), hx: 8 (over x, core).
Axes of the slice: x: 4, y: 4, z: 4, core: 2. Of those that a mesh axis runs over, the one named last changes fastest.
Arguments:
- queries: bfloat16 [2048, 4096], P('seq', 'hx'), may hold values from -6 to 6
- keys: bfloat16 [2048, 4096], P('seq', 'hx'), may hold values from -6 to 6
- values: bfloat16 [2048, 4096], P('seq', 'hx'), may hold values from -6 to 6
- log_decay: float32 [2048, 32], P('seq', 'hx'), may hold values from -1 to 0
- doc_ids: int32 [2048], P('seq'), may hold values from 0 to 3, as said below
- residual: bfloat16 [2048, 6144], P('seq'), may hold values from -6 to 6
- out_weight: bfloat16 [4096, 6144], P('hx'), may hold values from -0.09375 to 0.09375
- norm_gain: float32 [6144], replicated, may hold values from 0.1 to 1.9
- expert_ids: int32 [2048, 2], P('seq'), may hold values from 0 to 7, all different within a row; in each aligned block of 128 rows (0 to 127, 128 to 255, ...) at most 40 rows name the same one
- route_weight: float32 [2048, 2], P('seq'), may hold values from 0.2 to 1
- w_gate: bfloat16 [8, 6144, 4608], P('hx', None, 'seq'), may hold values from -0.078125 to 0.078125
- w_up: bfloat16 [8, 6144, 4608], P('hx', None, 'seq'), may hold values from -0.078125 to 0.078125
- w_down: bfloat16 [8, 4608, 6144], P('hx', 'seq'), may hold values from -0.09375 to 0.09375
Outputs:
- layer_out: bfloat16 [2048, 6144], P('seq', 'hx')
The draws below stay inside these ranges and needn't reach their ends.
Inputs may be any that keep to these rules, and one draw needn't show every extreme that they name: `expert_ids`: the two experts of a token differ; among the tokens of one sequence shard no expert is named more than 40 times, and some expert reaches 40. `doc_ids`: document numbers start at 0, never fall along the sequence, and rise by one at each of three positions.
All inputs are finite; a program needn't handle non-finite values.
Results may differ from the reference program's by a relative error of at most 0.022.
Values may be sent and summed in bfloat16 or wider, within the bound.
A program may use at most 128 MiB of HBM per device.

```python
import math
import jax
import jax.numpy as jnp
import numpy as np
from jax import lax

D = 6144
ATTN_GROUPS = 32
HS = 128
FF = 4608
TOK_DEV = 128
SPAN_LENGTH = 2048
EXPERTS = 8
CAP = 40
N_SEQ = 16


def draw_log_decay(key, part):
    key = jax.random.fold_in(key, 7)
    complete_lookup_vectors = jax.random.split(key, 6)
    fast_share = 0.5
    fast_heads = jax.random.uniform(complete_lookup_vectors[0], (ATTN_GROUPS,)) < fast_share
    fast_rate = jnp.exp(jax.random.uniform(complete_lookup_vectors[1], (ATTN_GROUPS,), minval=jnp.log(1.0 / 50.0), maxval=jnp.log(1.0 / 30.0)))
    slow_rate = jnp.exp(jax.random.uniform(complete_lookup_vectors[2], (ATTN_GROUPS,), minval=jnp.log(0.05), maxval=jnp.log(0.25))) * 2.3 / SPAN_LENGTH
    reference_forget_factor = jnp.where(fast_heads, fast_rate, slow_rate)
    noise_perturbation = jnp.exp(jax.random.uniform(complete_lookup_vectors[3], (SPAN_LENGTH, ATTN_GROUPS), minval=jnp.log(0.5), maxval=jnp.log(2.0)))
    segment_spans = jax.random.uniform(complete_lookup_vectors[4], (SPAN_LENGTH, ATTN_GROUPS)) < 2.0 / SPAN_LENGTH
    stack_level = jax.random.uniform(complete_lookup_vectors[5], (SPAN_LENGTH, ATTN_GROUPS), minval=0.22, maxval=0.69)
    closing_result_matrix = -(reference_forget_factor[None, :] * noise_perturbation + jnp.where(segment_spans, stack_level, 0.0))
    return closing_result_matrix.astype(jnp.float32)


def draw_doc_ids(key, part):
    key = jax.random.fold_in(key, 11)
    shuffled = jax.random.permutation(key, SPAN_LENGTH - 1)
    cut_points = shuffled[:3].astype(jnp.int32) + 1
    positions = jnp.arange(SPAN_LENGTH, dtype=jnp.int32)
    return jnp.sum((positions[:, None] >= cut_points[None, :]).astype(jnp.int32), axis=1).astype(jnp.int32)


def block_scale(own_key, shape, pieces, low, high):
    gain, own = 1.0, jax.random.fold_in(own_key, 6)
    for dim, shards_of in pieces:
        steps = jnp.exp(jax.random.uniform(jax.random.fold_in(own, dim), (shards_of,), jnp.float32, low / len(pieces), high / len(pieces)))
        gain = gain * jnp.repeat(steps, shape[dim] // shards_of).reshape([-1 if axis == dim else 1 for axis in range(len(shape))])
    return gain


def deal_out(rng, own, number, rows, number_of, top, reach, skew):
    order = jax.random.permutation(rng, number_of)
    packed, ordinary = portions_of(number_of, rows * top, reach, skew, True), portions_of(number_of, rows * top, reach, skew, False)
    places = jnp.arange(number_of)

    def named(sizes, rotation):
        used = int((sizes > 0).sum())
        fixed = max(1, used // 4)
        passed = fixed + (places - fixed + rotation * (used - fixed)) % max(1, number_of - fixed)
        return jnp.zeros((number_of,), jnp.int32).at[order[jnp.where(places < fixed, places, passed)]].set(jnp.asarray(sizes, jnp.int32))

    sizes = jnp.where(number % 4 == 0, named(packed, number // 4), named(ordinary, number - number // 4 - 1))
    mixed = jax.random.permutation(jax.random.fold_in(own, 3), number_of)
    giver, sink = mixed[0:number_of // 2 * 2:2], mixed[1:number_of // 2 * 2:2]
    slack = jnp.minimum(sizes[giver] - 1, reach - sizes[sink]) // 2
    slack = jnp.where((giver == order[0]) | (sink == order[0]) | (sizes[sink] == 0), 0, jnp.maximum(slack, 0))
    passed = jax.random.randint(jax.random.fold_in(own, 4), (number_of // 2,), 0, 1 << 20) % (slack + 1)
    sizes = sizes.at[giver].add(-passed).at[sink].add(passed)
    members = jnp.searchsorted(jnp.cumsum(sizes), jnp.arange(rows * top), side="right").astype(jnp.int32)
    listing = members.reshape(top, rows).T
    listing = listing[jax.random.permutation(jax.random.fold_in(own, 1), rows)]
    rotation = jax.random.randint(jax.random.fold_in(own, 2), (rows, 1), 0, top)
    return jnp.take_along_axis(listing, (jnp.arange(top)[None, :] + rotation) % top, axis=1)


def portions_of(count, total, bound, lean, full):
    weights = [(1 << 20) // math.isqrt(grade ** lean) + 1 for grade in range(1, count + 1)]
    largest = bound if full else min(bound, max(-(-total // count), total * weights[0] // sum(weights)))
    least = 1 if total - largest >= count - 1 else 0
    counts, rest = [largest] + [least] * (count - 1), total - largest - least * (count - 1)
    while rest > 0:
        candidates = [i for i in range(1, count) if counts[i] < largest] or [i for i in range(1, count) if counts[i] < bound]
        pool, budget = sum([weights[i] for i in candidates]), rest
        for i in candidates:
            more = min(bound - counts[i], max(1, budget * weights[i] // pool), rest)
            counts[i] = counts[i] + more
            rest = rest - more
    return np.array(counts)


def normal_values(own_key, dims, spread, most, pieces=(), kind=jnp.bfloat16):
    factor_of = block_scale(own_key, dims, pieces, -0.22, 0.18) if pieces else 1.0
    drawn = jax.random.normal(own_key, dims, jnp.float32) * spread * factor_of
    return jnp.minimum(jnp.maximum(drawn, -most), most).astype(kind)


def setup_inputs(seed: int = 0) -> dict:
    streams_of = jax.random.split(jax.random.key(seed), 14)
    queries = normal_values(streams_of[0], (SPAN_LENGTH, ATTN_GROUPS * HS), 1.0, 6.0, ((0, 16), (1, 8)))
    keys = normal_values(streams_of[1], (SPAN_LENGTH, ATTN_GROUPS * HS), 1.0, 6.0, ((0, 16), (1, 8)))
    values = normal_values(streams_of[2], (SPAN_LENGTH, ATTN_GROUPS * HS), 1.0, 6.0, ((0, 16), (1, 8)))
    log_decay = draw_log_decay(jax.random.fold_in(streams_of[13], 71), 0)
    doc_ids = draw_doc_ids(jax.random.fold_in(streams_of[13], 71), 0)
    residual = normal_values(streams_of[5], (SPAN_LENGTH, D), 1.0, 6.0, ((0, 16),))
    out_weight = normal_values(streams_of[6], (ATTN_GROUPS * HS, D), (ATTN_GROUPS * HS) ** -0.5, 0.09375, ((0, 8),))
    norm_gain = jnp.clip(1.0 + 0.18 * jax.random.normal(streams_of[7], (D,), jnp.float32), 0.1, 1.9)
    expert_ids_keys = jax.random.split(jax.random.fold_in(streams_of[8], 1), SPAN_LENGTH // TOK_DEV)
    expert_ids_turns = jax.random.permutation(jax.random.fold_in(streams_of[8], 3), SPAN_LENGTH // TOK_DEV)
    expert_ids = jax.vmap(lambda own, number: deal_out(jax.random.fold_in(streams_of[8], 2), own, number, TOK_DEV, EXPERTS, 2, CAP, 2))(expert_ids_keys, expert_ids_turns).reshape((SPAN_LENGTH, 2))
    route_weight = jnp.clip(0.2 + 0.8 * jax.random.uniform(streams_of[9], (SPAN_LENGTH, 2), jnp.float32) ** block_scale(streams_of[9], (SPAN_LENGTH, 2), ((0, 16),), -0.2, 0.2), 0.2, 1.0)
    w_gate = normal_values(streams_of[10], (EXPERTS, D, FF), D ** -0.5, 0.078125, ((0, 8), (2, 16)))
    w_up = normal_values(streams_of[11], (EXPERTS, D, FF), D ** -0.5, 0.078125, ((0, 8), (2, 16)))
    w_down = normal_values(streams_of[12], (EXPERTS, FF, D), FF ** -0.5, 0.09375, ((0, 8), (1, 16)))
    return {"queries": queries, "keys": keys, "values": values, "log_decay": log_decay, "doc_ids": doc_ids, "residual": residual, "out_weight": out_weight, "norm_gain": norm_gain, "expert_ids": expert_ids, "route_weight": route_weight, "w_gate": w_gate, "w_up": w_up, "w_down": w_down}


def reference(queries, keys, values, log_decay, doc_ids, residual, out_weight, norm_gain, expert_ids, route_weight, w_gate, w_up, w_down):
    query_f = queries.astype(jnp.float32).reshape(SPAN_LENGTH, ATTN_GROUPS, HS)
    key_f = keys.astype(jnp.float32).reshape(SPAN_LENGTH, ATTN_GROUPS, HS)
    value_f = values.astype(jnp.float32).reshape(SPAN_LENGTH, ATTN_GROUPS, HS)
    previous = jnp.concatenate([jnp.full((1,), -1, jnp.int32), doc_ids[:-1].astype(jnp.int32)])
    keep_factor = jnp.exp(log_decay) * (doc_ids == previous).astype(log_decay.dtype)[:, None]

    def advance(head_state, inputs):
        query_row, key_row, value_row, keep_row = inputs
        head_state = keep_row[:, None, None] * head_state + key_row[:, :, None] * value_row[:, None, :]
        return (head_state, jnp.einsum('hi,hij->hj', query_row, head_state, precision=lax.Precision.HIGHEST))
    initial = jnp.zeros((ATTN_GROUPS, HS, HS), query_f.dtype)
    _, head_out = lax.scan(advance, initial, (query_f, key_f, value_f, keep_factor))
    normed_heads = head_out * lax.rsqrt(lax.optimization_barrier(jnp.mean(head_out * head_out, axis=-1, keepdims=True)) + 1e-05)
    attn_in = normed_heads.reshape(SPAN_LENGTH, ATTN_GROUPS * HS).astype(jnp.bfloat16)
    hidden = residual.astype(jnp.float32) + jnp.dot(attn_in, out_weight, preferred_element_type=jnp.float32)
    normed = (hidden * lax.rsqrt(lax.optimization_barrier(jnp.mean(hidden * hidden, axis=-1, keepdims=True)) + 1e-06) * norm_gain).astype(jnp.bfloat16)
    moe_sum = jnp.zeros((SPAN_LENGTH, D), hidden.dtype)
    for expert in range(EXPERTS):
        chosen = expert_ids == expert
        used = jnp.any(chosen, axis=1)
        token_weight = lax.optimization_barrier(jnp.sum(jnp.where(chosen, route_weight, 0.0), axis=1))
        order = jnp.argsort(jnp.where(used, 0, 1).astype(jnp.int32), stable=True)[:N_SEQ * CAP]
        row_block = normed[order]
        gate_part = jnp.dot(row_block, w_gate[expert], preferred_element_type=jnp.float32)
        up_part = jnp.dot(row_block, w_up[expert], preferred_element_type=jnp.float32)
        act = (jax.nn.silu(gate_part) * up_part).astype(jnp.bfloat16)
        expert_out = jnp.dot(act, w_down[expert], preferred_element_type=jnp.float32)
        moe_sum = moe_sum.at[order].add(token_weight[order][:, None] * expert_out)
    return (hidden + moe_sum).astype(jnp.bfloat16)
```

```python
import functools
import jax
import jax.numpy as jnp
from jax import lax
from jax.experimental import pallas as pl
from jax.experimental.pallas import tpu as pltpu
from jax.sharding import PartitionSpec as P

MESH = pl.DeviceIdType.MESH
CAP = 40
SL = 8
W = 768
F = 288
ORDER = [(0, 0), (1, 0), (3, 0), (0, 1), (0, 3), (1, 1), (1, 3), (3, 1), (3, 3), (2, 0), (0, 2), (1, 2), (3, 2), (2, 1), (2, 3), (2, 2)]
SLOT = {r: i for i, r in enumerate(ORDER)}


def at(half, first, second):
    return SLOT[(first % 4, second % 4) if half == 0 else (second % 4, first % 4)]


class Mail:
    def __init__(self, send_sem, recv_sem):
        self.send_sem, self.recv_sem = send_sem, recv_sem
        self.number, self.sent = {}, []

    def make(self, key, src, dst, device):
        n = self.number.setdefault(key, len(self.number))
        return pltpu.make_async_remote_copy(
            src_ref=src, dst_ref=dst, send_sem=self.send_sem.at[n], recv_sem=self.recv_sem.at[n],
            device_id=device, device_id_type=MESH)

    def send(self, key, src, dst, device):
        copy = self.make(key, src, dst, device)
        copy.start()
        self.sent.append(copy)

    def arrived(self, key, dst, device):
        self.make(key, dst, dst, device).wait_recv()

    def drain(self):
        for copy in self.sent:
            copy.wait_send()


def ring(half, seq):
    y, z = seq // 4, seq % 4
    yp, ym = ((y + 1) % 4) * 4 + z, ((y + 3) % 4) * 4 + z
    zp, zm = y * 4 + (z + 1) % 4, y * 4 + (z + 3) % 4
    ids = (yp, ym, zp, zm) if half == 0 else (zp, zm, yp, ym)
    return [{"seq": i} for i in ids]


class Gather:
    def __init__(self, mail, x, half, seq):
        self.mail, self.x, self.half = mail, x, half
        self.fp, self.fm, self.sp, self.sm = ring(half, seq)

    def part(self, f, s, unit):
        lo, n = (4 * self.half, 4) if unit is None else (4 * self.half + 2 * unit, 2)
        return self.x.at[at(self.half, f, s), pl.ds(lo, n)]

    def push(self, f, s, unit, device, tf, ts, src=None):
        self.mail.send(("g", self.half, tf % 4, ts % 4, unit), self.part(f, s, unit) if src is None else src,
                       self.part(tf, ts, unit), device)

    def got(self, f, s, unit):
        self.mail.arrived(("g", self.half, f % 4, s % 4, unit), self.part(f, s, unit), self.fp)

    def across(self, f):
        self.push(f, 0, None, self.sp, f, 3)
        self.push(f, 0, None, self.sm, f, 1)

    def start(self):
        self.push(0, 0, None, self.fp, 3, 0)
        self.push(0, 0, None, self.fm, 1, 0)
        self.across(0)

    def first(self, f):
        self.got(f, 0, None)
        if f == 3:
            self.push(3, 0, 0, self.fp, 2, 0)
        else:
            self.push(1, 0, 1, self.fm, 2, 0)
        self.across(f)

    def first_far(self):
        self.got(2, 0, 0)
        self.got(2, 0, 1)
        self.across(2)

    def second(self, f):
        self.got(f, 3, None)
        self.push(f, 3, 0, self.sp, f, 2)
        self.got(f, 1, None)
        self.push(f, 1, 1, self.sm, f, 2)

    def second_far(self, f):
        self.got(f, 2, 0)
        self.got(f, 2, 1)


class Reduce:
    def __init__(self, mail, p, r1, r2, q1, q2, half, seq):
        self.mail, self.p, self.half = mail, p, half
        self.r1, self.r2, self.q1, self.q2 = r1, r2, q1, q2
        self.fp, self.fm, self.sp, self.sm = ring(half, seq)

    def unit(self, f, s, u):
        return self.p.at[at(self.half, f, s), pl.ds(4 * self.half + 2 * u, 2)]

    def push(self, key, src, dst, device):
        self.mail.send((self.half,) + key, src, dst, device)

    def got(self, key, dst):
        self.mail.arrived((self.half,) + key, dst, self.fp)
        return dst

    def add(self, f, s, u, *others):
        mine = self.unit(f, s, u)
        for k in range(2):
            total = mine[k].astype(jnp.float32)
            for other in others:
                total += other[k].astype(jnp.float32)
            mine[k] = total.astype(jnp.bfloat16)

    def start(self, f):
        h = self.half
        self.push(("r1", f, 0), self.unit(f, 2, 0), self.r1.at[h, f, 0], self.sp)
        self.push(("r1", f, 1), self.unit(f, 2, 1), self.r1.at[h, f, 1], self.sm)
        self.push(("r2", f, 0, 1), self.unit(f, 1, 1), self.r2.at[h, f, 0, 1], self.sp)
        self.push(("r2", f, 1, 0), self.unit(f, 3, 0), self.r2.at[h, f, 1, 0], self.sm)

    def middle(self, f):
        h = self.half
        self.add(f, 1, 0, self.got(("r1", f, 0), self.r1.at[h, f, 0]))
        self.push(("r2", f, 0, 0), self.unit(f, 1, 0), self.r2.at[h, f, 0, 0], self.sp)
        self.add(f, 3, 1, self.got(("r1", f, 1), self.r1.at[h, f, 1]))
        self.push(("r2", f, 1, 1), self.unit(f, 3, 1), self.r2.at[h, f, 1, 1], self.sm)

    def end(self, f):
        h = self.half
        for u in (0, 1):
            self.add(f, 0, u, self.got(("r2", f, 0, u), self.r2.at[h, f, 0, u]),
                     self.got(("r2", f, 1, u), self.r2.at[h, f, 1, u]))
        if f == 2:
            self.push(("q1", 0), self.unit(2, 0, 0), self.q1.at[h, 0], self.fp)
            self.push(("q1", 1), self.unit(2, 0, 1), self.q1.at[h, 1], self.fm)
        if f == 1:
            self.push(("q2", 0, 1), self.unit(1, 0, 1), self.q2.at[h, 0, 1], self.fp)
            self.add(1, 0, 0, self.got(("q1", 0), self.q1.at[h, 0]))
            self.push(("q2", 0, 0), self.unit(1, 0, 0), self.q2.at[h, 0, 0], self.fp)
        if f == 3:
            self.push(("q2", 1, 0), self.unit(3, 0, 0), self.q2.at[h, 1, 0], self.fm)
            self.add(3, 0, 1, self.got(("q1", 1), self.q1.at[h, 1]))
            self.push(("q2", 1, 1), self.unit(3, 0, 1), self.q2.at[h, 1, 1], self.fm)

    def last(self, u, out):
        h = self.half
        a = self.got(("q2", 0, u), self.q2.at[h, 0, u])
        b = self.got(("q2", 1, u), self.q2.at[h, 1, u])
        mine = self.unit(0, 0, u)
        for k in range(2):
            total = mine[k].astype(jnp.float32) + a[k].astype(jnp.float32) + b[k].astype(jnp.float32)
            out[4 * h + 2 * u + k] = total.astype(out.dtype)


def expert_kernel(x_in, wg_in, wu_in, wd_in, out, x, p, wg, wu, wd, acc_g, acc_u, act, r1, r2, q1, q2,
                  load_sem, send_sem, recv_sem):
    seq = lax.axis_index("seq")
    loads = [pltpu.make_async_copy(wg_in, wg, load_sem.at[0]), pltpu.make_async_copy(wu_in, wu, load_sem.at[1])]
    for k in range(SL):
        loads.append(pltpu.make_async_copy(wd_in.at[:, pl.ds(k * W, W)], wd.at[k], load_sem.at[2 + k]))
    own = pltpu.make_async_copy(x_in, x.at[0], load_sem.at[2 + SL])
    own.start()
    barrier = pltpu.get_barrier_semaphore()
    for device in ring(0, seq):
        pl.semaphore_signal(barrier, inc=1, device_id=device, device_id_type=MESH)
    pl.semaphore_wait(barrier, 4)
    own.wait()

    mail = Mail(send_sem, recv_sem)
    gathers = [Gather(mail, x, half, seq) for half in (0, 1)]
    reduces = [Reduce(mail, p, r1, r2, q1, q2, half, seq) for half in (0, 1)]

    def compute(group):
        rows = pl.ds(4 * group, 4)
        acc_g[...] = jnp.zeros_like(acc_g)
        acc_u[...] = jnp.zeros_like(acc_u)

        def up(k, _):
            block = x[rows, k].astype(jnp.float32).reshape(4 * CAP, W).astype(jnp.bfloat16)
            acc_g[...] += jnp.dot(block, wg[k], preferred_element_type=jnp.float32)
            acc_u[...] += jnp.dot(block, wu[k], preferred_element_type=jnp.float32)
            return 0

        lax.fori_loop(0, SL, up, 0)
        gate = acc_g[...]
        act[...] = (gate / (1.0 + jnp.exp(-gate)) * acc_u[...]).astype(jnp.bfloat16)

        def down(k, _):
            block = jnp.dot(act[...], wd[k], preferred_element_type=jnp.float32)
            p[rows, k] = block.reshape(4, CAP, W).astype(jnp.bfloat16)
            return 0

        lax.fori_loop(0, SL, down, 0)

    for g in gathers:
        g.start()
    for copy in loads:
        copy.start()
    for f in (3, 1):
        for g in gathers:
            g.first(f)
    for g in gathers:
        g.second(0)
    for copy in loads:
        copy.wait()
    compute(0)
    for g in gathers:
        g.first_far()
    for f in (3, 1):
        for g in gathers:
            g.second(f)
    compute(1)
    for g in gathers:
        g.second(2)
    for g in gathers:
        g.second_far(0)
    for f in (3, 1):
        for g in gathers:
            g.second_far(f)
    compute(2)
    for g in gathers:
        g.second_far(2)
    compute(3)

    def each(step, f):
        for r in reduces:
            getattr(r, step)(f)

    each("start", 2)
    each("start", 1)
    each("middle", 2)
    each("start", 3)
    each("middle", 1)
    each("end", 2)
    each("start", 0)
    each("middle", 3)
    each("end", 1)
    each("middle", 0)
    each("end", 3)
    each("end", 0)
    for u in (0, 1):
        for r in reduces:
            r.last(u, out)
    mail.drain()


N_MAIL = 40 + 48 + 12


def experts(x, w_gate, w_up, w_down):
    vmem = pl.BlockSpec(memory_space=pltpu.VMEM)
    hbm = pl.BlockSpec(memory_space=pl.ANY)
    bf = jnp.bfloat16
    return pl.pallas_call(
        expert_kernel,
        out_shape=jax.ShapeDtypeStruct((SL, CAP, W), bf),
        in_specs=[vmem, hbm, hbm, hbm],
        out_specs=vmem,
        scratch_shapes=[
            pltpu.VMEM((16, SL, CAP, W), bf),
            pltpu.VMEM((16, SL, CAP, W), bf),
            pltpu.VMEM((SL, W, F), bf),
            pltpu.VMEM((SL, W, F), bf),
            pltpu.VMEM((SL, F, W), bf),
            pltpu.VMEM((4 * CAP, F), jnp.float32),
            pltpu.VMEM((4 * CAP, F), jnp.float32),
            pltpu.VMEM((4 * CAP, F), bf),
            pltpu.VMEM((2, 4, 2, 2, CAP, W), bf),
            pltpu.VMEM((2, 4, 2, 2, 2, CAP, W), bf),
            pltpu.VMEM((2, 2, 2, CAP, W), bf),
            pltpu.VMEM((2, 2, 2, 2, CAP, W), bf),
            pltpu.SemaphoreType.DMA((3 + SL,)),
            pltpu.SemaphoreType.DMA((N_MAIL,)),
            pltpu.SemaphoreType.DMA((N_MAIL,)),
        ],
        compiler_params=pltpu.CompilerParams(collective_id=1, has_side_effects=True, vmem_limit_bytes=60 * 2**20),
        name="experts",
    )(x, w_gate.reshape(SL, W, F), w_up.reshape(SL, W, F), w_down)

HS = 128


def prefix(shard, axis, join, neutral):
    place = lax.axis_index(axis)
    gathered = jax.tree.map(
        lambda a, kind: lax.all_gather(a.astype(kind), axis),
        shard,
        (jnp.bfloat16, jnp.bfloat16, jnp.bfloat16, jnp.bfloat16),
    )
    state = jax.tree.map(lambda a, e: jnp.zeros_like(a) + jnp.asarray(e, a.dtype), shard, neutral)

    def one(turn, state):
        return join(
            state,
            jax.tree.map(
                lambda a, own: lax.dynamic_index_in_dim(a, turn, 0, False).astype(own.dtype),
                gathered,
                shard,
            ),
        )

    return lax.fori_loop(0, place, one, state)


def link_states(earlier, later):
    through_one, state_one, first_one, last_one = earlier
    through_two, state_two, first_two, last_two = later
    passes = ((last_one < 0) | (first_two < 0) | (last_one == first_two)).astype(jnp.float32)
    through = through_one * through_two * passes
    head_state = passes * through_two[:, None, None] * state_one + state_two
    first_doc = jnp.where(first_one >= 0, first_one, first_two)
    last_doc = jnp.where(last_two >= 0, last_two, last_one)
    return (through, head_state, first_doc, last_doc)


def shards(
    queries,
    keys,
    values,
    log_decay,
    doc_ids,
    residual,
    out_weight,
    norm_gain,
    expert_ids,
    route_weight,
    w_gate,
    w_up,
    w_down,
):
    tok_count = queries.shape[0]
    heads_local = log_decay.shape[1]
    query_heads = queries.reshape(tok_count, heads_local, HS)
    key_heads = keys.reshape(tok_count, heads_local, HS)
    value_float = values.reshape(tok_count, heads_local, HS).astype(jnp.float32)
    log_cum = jnp.cumsum(log_decay, axis=0)
    positions = jnp.arange(tok_count)
    allowed = (positions[:, None] >= positions[None, :]) & (doc_ids[:, None] == doc_ids[None, :])
    exponent = jnp.where(allowed[None], log_cum.T[:, :, None] - log_cum.T[:, None, :], -jnp.inf)
    scores = jnp.einsum("thd,shd->hts", query_heads, key_heads, preferred_element_type=jnp.float32)
    intra = jnp.einsum(
        "hts,shd->thd", scores * jnp.exp(exponent), value_float, precision=lax.Precision.HIGHEST
    )
    first_doc = doc_ids[0]
    last_doc = doc_ids[tok_count - 1]
    end_weight = (
        jnp.exp(log_cum[tok_count - 1][None, :] - log_cum)
        * (doc_ids == last_doc).astype(jnp.float32)[:, None]
    )
    key_weighted = key_heads.astype(jnp.float32) * end_weight[:, :, None]
    head_state = jnp.einsum(
        "shi,shj->hij", key_weighted, value_float, precision=lax.Precision.HIGHEST
    )
    through = jnp.exp(log_cum[tok_count - 1]) * (first_doc == last_doc).astype(jnp.float32)
    first_float = jnp.full((1,), first_doc).astype(jnp.float32)
    last_float = jnp.full((1,), last_doc).astype(jnp.float32)
    identity = (
        jnp.ones((heads_local,), jnp.float32),
        jnp.zeros_like(head_state),
        jnp.full((1,), -1.0, jnp.float32),
        jnp.full((1,), -1.0, jnp.float32),
    )
    carried = prefix((through, head_state, first_float, last_float), "seq", link_states, identity)
    incoming = carried[1]
    before_doc = carried[3]
    entry_gate = (before_doc[0] == first_float[0]).astype(jnp.float32)
    carry_weight = (
        jnp.exp(log_cum) * (doc_ids == first_doc).astype(jnp.float32)[:, None] * entry_gate
    )
    query_weighted = query_heads.astype(jnp.float32) * carry_weight[:, :, None]
    carried_out = jnp.einsum(
        "thi,hij->thj", query_weighted, incoming, precision=lax.Precision.HIGHEST
    )
    head_out = intra + carried_out
    normed_heads = head_out * lax.rsqrt(
        jnp.mean(head_out * head_out, axis=-1, keepdims=True) + 1e-05
    )
    attn_in = normed_heads.reshape(tok_count, heads_local * HS).astype(jnp.bfloat16)
    expert_count = lax.axis_size("hx")
    capacity = tok_count * 5 // (2 * expert_count)
    flat_ids = expert_ids.reshape(-1)
    choice_count = flat_ids.shape[0]
    one_hot = (flat_ids[:, None] == jnp.arange(expert_count)[None, :]).astype(jnp.int32)
    rank_before = jnp.cumsum(one_hot, axis=0) - one_hot
    slot_index = flat_ids * capacity + jnp.sum(rank_before * one_hot, axis=1)
    token_of = jnp.arange(choice_count) // 2
    slot_match = slot_index[None, :] == jnp.arange(expert_count * capacity)[:, None]
    slot_valid = jnp.any(slot_match, axis=1)
    slot_token = jnp.sum(jnp.where(slot_match, token_of[None, :], 0), axis=1)
    expert_index = lax.axis_index("hx")
    first_slot = slot_index[0::2]
    second_slot = slot_index[1::2]
    row_block = jnp.where(slot_valid[:, None], attn_in[slot_token], jnp.zeros((), jnp.bfloat16))
    attn_slots = lax.psum_scatter(
        jnp.dot(row_block, out_weight, preferred_element_type=jnp.float32).astype(jnp.bfloat16),
        "hx",
        scatter_dimension=0,
        tiled=True,
    ).astype(jnp.float32)
    my_tokens = lax.dynamic_slice_in_dim(slot_token, expert_index * capacity, capacity)
    hidden_slots = residual[my_tokens].astype(jnp.float32) + attn_slots
    normed = (
        hidden_slots
        * lax.rsqrt(jnp.mean(hidden_slots * hidden_slots, axis=-1, keepdims=True) + 1e-06)
        * norm_gain
    ).astype(jnp.bfloat16)
    blocks = normed.reshape(capacity, SL, W).transpose(1, 0, 2)
    expert_out = experts(blocks, w_gate[0], w_up[0], w_down[0]).transpose(1, 0, 2).reshape(capacity, SL * W)
    back_hidden, back_expert = (
        lax.all_to_all(
            hidden_slots.astype(jnp.bfloat16), "hx", split_axis=1, concat_axis=0, tiled=True
        ).astype(hidden_slots.dtype),
        lax.all_to_all(
            expert_out.astype(jnp.bfloat16), "hx", split_axis=1, concat_axis=0, tiled=True
        ).astype(expert_out.dtype),
    )
    layer_out = (
        back_hidden[first_slot]
        + route_weight[:, 0:1] * back_expert[first_slot]
        + route_weight[:, 1:2] * back_expert[second_slot]
    )
    return layer_out.astype(jnp.bfloat16)


def solution(mesh):
    return jax.shard_map(
        shards,
        mesh=mesh,
        in_specs=(
            P("seq", "hx"),
            P("seq", "hx"),
            P("seq", "hx"),
            P("seq", "hx"),
            P("seq"),
            P("seq", None),
            P("hx", None),
            P(),
            P("seq", None),
            P("seq", None),
            P("hx", None, "seq"),
            P("hx", None, "seq"),
            P("hx", "seq", None),
        ),
        out_specs=P("seq", "hx"),
        check_vma=False,
    )
```

```python
import jax
import jax.numpy as jnp
from jax import lax
from jax.experimental import pallas as pl
from jax.experimental.pallas import tpu as pltpu
from jax.sharding import PartitionSpec as P

MESH = pl.DeviceIdType.MESH
CAP = 40
HS = 128
HEADS = 4
T = 128
N_SEQ = 16
SL = 8
W = 768
F = 288
ORDER = [(0, 0), (1, 0), (3, 0), (0, 1), (0, 3), (1, 1), (1, 3), (3, 1), (3, 3), (2, 0), (0, 2), (1, 2), (3, 2), (2, 1), (2, 3), (2, 2)]
SLOT = {r: i for i, r in enumerate(ORDER)}


def at(half, first, second):
    return SLOT[(first % 4, second % 4) if half == 0 else (second % 4, first % 4)]


class Mail:
    def __init__(self, send_sem, recv_sem):
        self.send_sem, self.recv_sem = send_sem, recv_sem
        self.number, self.sent = {}, []

    def make(self, key, src, dst, device):
        n = self.number.setdefault(key, len(self.number))
        return pltpu.make_async_remote_copy(
            src_ref=src, dst_ref=dst, send_sem=self.send_sem.at[n], recv_sem=self.recv_sem.at[n],
            device_id=device, device_id_type=MESH)

    def send(self, key, src, dst, device):
        copy = self.make(key, src, dst, device)
        copy.start()
        self.sent.append(copy)

    def arrived(self, key, dst, device):
        self.make(key, dst, dst, device).wait_recv()

    def drain(self):
        for copy in self.sent:
            copy.wait_send()


def ring(half, seq):
    y, z = seq // 4, seq % 4
    yp, ym = ((y + 1) % 4) * 4 + z, ((y + 3) % 4) * 4 + z
    zp, zm = y * 4 + (z + 1) % 4, y * 4 + (z + 3) % 4
    ids = (yp, ym, zp, zm) if half == 0 else (zp, zm, yp, ym)
    return [{"seq": i} for i in ids]


class Gather:
    def __init__(self, mail, x, half, seq):
        self.mail, self.x, self.half = mail, x, half
        self.fp, self.fm, self.sp, self.sm = ring(half, seq)

    def part(self, f, s, unit):
        lo, n = (4 * self.half, 4) if unit is None else (4 * self.half + 2 * unit, 2)
        return self.x.at[at(self.half, f, s), pl.ds(lo, n)]

    def push(self, f, s, unit, device, tf, ts, src=None):
        self.mail.send(("g", self.half, tf % 4, ts % 4, unit), self.part(f, s, unit) if src is None else src,
                       self.part(tf, ts, unit), device)

    def got(self, f, s, unit):
        self.mail.arrived(("g", self.half, f % 4, s % 4, unit), self.part(f, s, unit), self.fp)

    def across(self, f):
        self.push(f, 0, None, self.sp, f, 3)
        self.push(f, 0, None, self.sm, f, 1)

    def start(self):
        self.push(0, 0, None, self.fp, 3, 0)
        self.push(0, 0, None, self.fm, 1, 0)
        self.across(0)

    def first(self, f):
        self.got(f, 0, None)
        if f == 3:
            self.push(3, 0, 0, self.fp, 2, 0)
        else:
            self.push(1, 0, 1, self.fm, 2, 0)
        self.across(f)

    def first_far(self):
        self.got(2, 0, 0)
        self.got(2, 0, 1)
        self.across(2)

    def second(self, f):
        self.got(f, 3, None)
        self.push(f, 3, 0, self.sp, f, 2)
        self.got(f, 1, None)
        self.push(f, 1, 1, self.sm, f, 2)

    def second_far(self, f):
        self.got(f, 2, 0)
        self.got(f, 2, 1)


class Reduce:
    def __init__(self, mail, p, r1, r2, q1, q2, half, seq):
        self.mail, self.p, self.half = mail, p, half
        self.r1, self.r2, self.q1, self.q2 = r1, r2, q1, q2
        self.fp, self.fm, self.sp, self.sm = ring(half, seq)

    def unit(self, f, s, u):
        return self.p.at[at(self.half, f, s), pl.ds(4 * self.half + 2 * u, 2)]

    def push(self, key, src, dst, device):
        self.mail.send((self.half,) + key, src, dst, device)

    def got(self, key, dst):
        self.mail.arrived((self.half,) + key, dst, self.fp)
        return dst

    def add(self, f, s, u, *others):
        mine = self.unit(f, s, u)
        for k in range(2):
            total = mine[k].astype(jnp.float32)
            for other in others:
                total += other[k].astype(jnp.float32)
            mine[k] = total.astype(jnp.bfloat16)

    def start(self, f):
        h = self.half
        self.push(("r1", f, 0), self.unit(f, 2, 0), self.r1.at[h, f, 0], self.sp)
        self.push(("r1", f, 1), self.unit(f, 2, 1), self.r1.at[h, f, 1], self.sm)
        self.push(("r2", f, 0, 1), self.unit(f, 1, 1), self.r2.at[h, f, 0, 1], self.sp)
        self.push(("r2", f, 1, 0), self.unit(f, 3, 0), self.r2.at[h, f, 1, 0], self.sm)

    def middle(self, f):
        h = self.half
        self.add(f, 1, 0, self.got(("r1", f, 0), self.r1.at[h, f, 0]))
        self.push(("r2", f, 0, 0), self.unit(f, 1, 0), self.r2.at[h, f, 0, 0], self.sp)
        self.add(f, 3, 1, self.got(("r1", f, 1), self.r1.at[h, f, 1]))
        self.push(("r2", f, 1, 1), self.unit(f, 3, 1), self.r2.at[h, f, 1, 1], self.sm)

    def end(self, f):
        h = self.half
        for u in (0, 1):
            self.add(f, 0, u, self.got(("r2", f, 0, u), self.r2.at[h, f, 0, u]),
                     self.got(("r2", f, 1, u), self.r2.at[h, f, 1, u]))
        if f == 2:
            self.push(("q1", 0), self.unit(2, 0, 0), self.q1.at[h, 0], self.fp)
            self.push(("q1", 1), self.unit(2, 0, 1), self.q1.at[h, 1], self.fm)
        if f == 1:
            self.push(("q2", 0, 1), self.unit(1, 0, 1), self.q2.at[h, 0, 1], self.fp)
            self.add(1, 0, 0, self.got(("q1", 0), self.q1.at[h, 0]))
            self.push(("q2", 0, 0), self.unit(1, 0, 0), self.q2.at[h, 0, 0], self.fp)
        if f == 3:
            self.push(("q2", 1, 0), self.unit(3, 0, 0), self.q2.at[h, 1, 0], self.fm)
            self.add(3, 0, 1, self.got(("q1", 1), self.q1.at[h, 1]))
            self.push(("q2", 1, 1), self.unit(3, 0, 1), self.q2.at[h, 1, 1], self.fm)

    def last(self, u, out):
        h = self.half
        a = self.got(("q2", 0, u), self.q2.at[h, 0, u])
        b = self.got(("q2", 1, u), self.q2.at[h, 1, u])
        mine = self.unit(0, 0, u)
        for k in range(2):
            total = mine[k].astype(jnp.float32) + a[k].astype(jnp.float32) + b[k].astype(jnp.float32)
            out[4 * h + 2 * u + k] = total.astype(out.dtype)


def iota(shape, dim):
    return lax.broadcasted_iota(jnp.int32, shape, dim)


def f32(a):
    return a.astype(jnp.float32)


def bf16(a):
    return a.astype(jnp.bfloat16)


def dot(a, b, ca=1, cb=0, **kw):
    return lax.dot_general(a, b, (((ca,), (cb,)), ((), ())), preferred_element_type=jnp.float32, **kw)


def dispatch(ids):
    experts = iota((SL, T), 0)
    named = (ids[0:1, :] == experts) | (ids[1:2, :] == experts)
    before = bf16(jnp.where(iota((T, T), 0) < iota((T, T), 1), 1.0, 0.0))
    rank = dot(bf16(jnp.where(named, 1.0, 0.0)), before)
    slot = f32(iota((CAP, T), 0))
    chosen = f32(jnp.where(named, 1.0, 0.0))
    return [jnp.where(rank[e : e + 1, :] == slot, 1.0, 0.0) * chosen[e : e + 1, :] for e in range(SL)]


def greet(seq, x, c):
    others = [{"seq": (seq + d) % N_SEQ} for d in range(1, N_SEQ)]
    others += [{"hx": (2 * x + c + d) % SL} for d in range(1, SL)]
    barrier = pltpu.get_barrier_semaphore()
    for device in others:
        pl.semaphore_signal(barrier, inc=1, device_id=device, device_id_type=MESH)
    pl.semaphore_wait(barrier, len(others))


def local_attention(q, k, v, decay, docs, states, head_out, carry):
    doc_row = jnp.broadcast_to(f32(docs[...]), (T, T))
    doc_col = doc_row.T
    allowed = (iota((T, T), 0) >= iota((T, T), 1)) & (doc_row == doc_col)
    upto = f32(jnp.where(iota((T, T), 0) <= iota((T, T), 1), 1.0, 0.0))
    rows = jnp.concatenate([decay[...], jnp.zeros((8 - HEADS, T), jnp.float32)], axis=0)
    sums = dot(rows, upto, precision=lax.Precision.HIGHEST)
    first, last = doc_col[0:1, :], doc_col[T - 1 : T, :]
    row = iota((16, HS), 0)
    for h in range(HEADS):
        lanes = slice(h * HS, (h + 1) * HS)
        across = jnp.broadcast_to(sums[h : h + 1, :], (T, T))
        down = across.T
        fade = jnp.where(allowed, jnp.exp(jnp.where(allowed, down - across, 0.0)), 0.0)
        scores = dot(q[:, lanes], k[:, lanes], 1, 1)
        head_out[h] = dot(bf16(scores * fade), v[:, lanes])
        total = down[T - 1 : T, :]
        to_end = jnp.where(doc_col == last, jnp.exp(total - down), 0.0)
        state = bf16(dot(bf16(f32(k[:, lanes]) * to_end), v[:, lanes], 0, 0))
        carry[h] = bf16(f32(q[:, lanes]) * jnp.where(doc_col == first, jnp.exp(down), 0.0))
        high = f32(bf16(total))
        mid = f32(bf16(total - high))
        low = total - high - mid
        facts = jnp.where(row == 0, high, jnp.where(row == 1, mid, jnp.where(row == 2, low, jnp.where(row == 3, first, last))))
        for part in range(4):
            states[4 * h + part, 0:32] = state[32 * part : 32 * (part + 1)]
            states[4 * h + part, 32:48] = bf16(facts)


def carry_states(mail, seq, states, arrived, entering, incoming, meanwhile):
    for d in range(1, N_SEQ):
        mail.send(("s", d), states.at[(seq + d) % N_SEQ], arrived.at[seq], {"seq": (seq + d) % N_SEQ})
    arrived[seq] = states[seq]
    meanwhile()
    for d in range(1, N_SEQ):
        mail.arrived(("s", d), arrived.at[(seq + N_SEQ - d) % N_SEQ], {"seq": (seq + d) % N_SEQ})
    state = jnp.zeros((32, HS), jnp.float32)
    before = jnp.full((1, HS), -1.0, jnp.float32)
    for s in range(N_SEQ):
        facts = f32(arrived[s, 32:48])
        log_total = facts[0:1] + facts[1:2] + facts[2:3]
        first, last = facts[3:4], facts[4:5]
        state = state * jnp.where(before == first, 1.0, 0.0)
        entering[s] = bf16(state)
        state = state * jnp.where(first == last, jnp.exp(log_total), 0.0) + f32(arrived[s, 0:32])
        before = last
    for d in range(1, N_SEQ):
        mail.send(("c", d), entering.at[(seq + d) % N_SEQ], incoming.at[seq], {"seq": (seq + d) % N_SEQ})
    incoming[seq] = entering[seq]
    for d in range(1, N_SEQ):
        mail.arrived(("c", d), incoming.at[(seq + N_SEQ - d) % N_SEQ], {"seq": (seq + d) % N_SEQ})


def attention_rows(head_out, carry, incoming, attn):
    for h in range(HEADS):
        state = incoming[4 * h : 4 * h + 4].reshape(HS, HS)
        out = head_out[h] + dot(carry[h], state)
        mean = jnp.mean(out * out, axis=1, keepdims=True)
        attn[:, h * HS : (h + 1) * HS] = bf16(out * lax.rsqrt(mean + 1e-05))


HALF = T // 2


def project(mail, x, c, attn, wo, to_twin, from_twin, part, r1, r2, residual, hidden):
    twin = {"hx": 2 * x + 1 - c}
    up, down = {"hx": 2 * ((x + 1) % 4) + c}, {"hx": 2 * ((x + 3) % 4) + c}
    order = (2, 1, 3, 0)

    def send_twin(dx):
        to_twin[dx] = bf16(dot(attn[...], wo[2 * dx + 1 - c])).reshape(2, HALF, W)
        mail.send(("t", dx), to_twin.at[dx], from_twin.at[dx], twin)

    def both(dx):
        mine = dot(attn[...], wo[2 * dx + c]).reshape(2, HALF, W)
        mail.arrived(("t", dx), from_twin.at[dx], twin)
        return mine + f32(from_twin[dx])

    send_twin(2)
    send_twin(1)
    part[2] = bf16(both(2))
    mail.send(("p1", 0), part.at[2, 0], r1.at[0], up)
    mail.send(("p1", 1), part.at[2, 1], r1.at[1], down)
    send_twin(3)
    mine = both(1)
    part[1, 1] = bf16(mine[1])
    mail.send(("p2", 0, 1), part.at[1, 1], r2.at[0, 1], up)
    send_twin(0)
    mail.arrived(("p1", 0), r1.at[0], up)
    part[1, 0] = bf16(mine[0] + f32(r1[0]))
    mail.send(("p2", 0, 0), part.at[1, 0], r2.at[0, 0], up)
    mine = both(3)
    part[3, 0] = bf16(mine[0])
    mail.send(("p2", 1, 0), part.at[3, 0], r2.at[1, 0], down)
    mail.arrived(("p1", 1), r1.at[1], up)
    part[3, 1] = bf16(mine[1] + f32(r1[1]))
    mail.send(("p2", 1, 1), part.at[3, 1], r2.at[1, 1], down)
    mine = both(0)
    for u in (1, 0):
        rows = slice(u * HALF, (u + 1) * HALF)
        mail.arrived(("p2", 0, u), r2.at[0, u], up)
        mail.arrived(("p2", 1, u), r2.at[1, u], up)
        hidden[rows, :] = f32(residual[rows, :]) + mine[u] + f32(r2[0, u]) + f32(r2[1, u])


WS = W + 128


class Cross:
    def __init__(self, send_sem, recv_sem, x, c):
        self.send_sem, self.recv_sem, self.x, self.c, self.sent = send_sem, recv_sem, x, c, []

    def make(self, dx, to, own, src, dst):
        return pltpu.make_async_remote_copy(
            src_ref=src, dst_ref=dst, send_sem=self.send_sem.at[2 * dx + to], recv_sem=self.recv_sem.at[2 * dx + own],
            device_id={"hx": 2 * ((self.x + dx) % 4) + to}, device_id_type=MESH)

    def send(self, dx, to, src, dst):
        copy = self.make(dx, to, self.c, src, dst)
        copy.start()
        self.sent.append(copy)

    def arrived(self, dx, own, dst):
        self.make(dx, own, own, dst, dst).wait_recv()

    def drain(self):
        for copy in self.sent:
            copy.wait_send()


def rows_to_experts(cross, x, c, hidden, pick, out, slots):
    square = jnp.sum(hidden[...] * hidden[...], axis=1, keepdims=True)
    high = f32(bf16(square))
    facts = jnp.where(iota((T, 128), 1) < 64, high, square - high)
    rows = jnp.concatenate([bf16(hidden[...]), bf16(facts)], axis=1)
    for dx in (2, 1, 3):
        for to in (0, 1):
            out[2 * dx + to] = bf16(dot(pick[2 * ((x + dx) % 4) + to], rows))
            cross.send(dx, to, out.at[2 * dx + to], slots.at[2 * (4 - dx) + c])
    out[0] = bf16(dot(pick[2 * x + 1 - c], rows))
    cross.send(0, 1 - c, out.at[0], slots.at[c])
    slots[c] = bf16(dot(pick[2 * x + c], rows))
    cross.arrived(0, 1 - c, slots.at[1 - c])
    for dx in (1, 3, 2):
        for own in (0, 1):
            cross.arrived(dx, own, slots.at[2 * (4 - dx) + own])


def norm_rows(x, slots, gain, rows):
    square = sum(f32(slots[k, :, W:WS]) for k in range(SL))
    mean = (square[:, 0:1] + square[:, 64:65]) * (1.0 / (SL * W))
    scale = lax.rsqrt(mean + 1e-06)
    for k in range(SL):
        rows[0, k] = bf16(f32(slots[k, :, 0:W]) * scale * gain[pl.ds((2 * x + k) % SL, 1), :])


def run_experts(mail, seq, rows, p, wg, wu, wd, acc_g, acc_u, act, r1, r2, q1, q2, loads, out, finish):
    gathers = [Gather(mail, rows, half, seq) for half in (0, 1)]
    reduces = [Reduce(mail, p, r1, r2, q1, q2, half, seq) for half in (0, 1)]

    def compute(group):
        blocks = pl.ds(4 * group, 4)
        acc_g[...] = jnp.zeros_like(acc_g)
        acc_u[...] = jnp.zeros_like(acc_u)

        def up(k, _):
            block = bf16(f32(rows[blocks, k]).reshape(4 * CAP, W))
            acc_g[...] += dot(block, wg[k], 1, 1)
            acc_u[...] += dot(block, wu[k], 1, 1)
            return 0

        lax.fori_loop(0, SL, up, 0)
        gate = acc_g[...]
        act[...] = bf16(gate / (1.0 + jnp.exp(-gate)) * acc_u[...])

        def down(k, _):
            p[blocks, k] = bf16(dot(act[...], wd[k]).reshape(4, CAP, W))
            return 0

        lax.fori_loop(0, SL, down, 0)

    for g in gathers:
        g.start()
    for f in (3, 1):
        for g in gathers:
            g.first(f)
    for g in gathers:
        g.second(0)
    for copy in loads:
        copy.wait()
    compute(0)
    for g in gathers:
        g.first_far()
    for f in (3, 1):
        for g in gathers:
            g.second(f)
    compute(1)
    for g in gathers:
        g.second(2)
    for g in gathers:
        g.second_far(0)
    for f in (3, 1):
        for g in gathers:
            g.second_far(f)
    compute(2)
    for g in gathers:
        g.second_far(2)
    compute(3)

    def each(step, f):
        for r in reduces:
            getattr(r, step)(f)

    each("start", 2)
    each("start", 1)
    each("middle", 2)
    each("start", 3)
    each("middle", 1)
    each("end", 2)
    each("start", 0)
    each("middle", 3)
    each("end", 1)
    each("middle", 0)
    each("end", 3)
    each("end", 0)
    for u in (1, 0):
        for half in (1, 0):
            reduces[half].last(u, out)
            finish(2 * half + u)


def layer_kernel(q, k, v, decay, docs, residual_in, wo_in, gain, ids, weights, wg_in, wu_in, wd_in, result,
                 wo, residual, pick, states, arrived, entering, incoming, head_out, carry, attn,
                 to_twin, from_twin, part, s1, s2, hidden, slot_out, slots,
                 rows, p, wg, wu, wd, acc_g, acc_u, act, r1, r2, q1, q2, done, back,
                 load_sem, send_sem, recv_sem, out_send, out_recv, back_send, back_recv):
    seq, hx = lax.axis_index("seq"), lax.axis_index("hx")
    x, c = hx // 2, hx % 2

    def lanes(n):
        return pl.ds(pl.multiple_of(n * W, W), W)

    front = [pltpu.make_async_copy(wo_in.at[:, lanes((2 * x + n) % SL)], wo.at[n], load_sem.at[n]) for n in range(SL)]
    front.append(pltpu.make_async_copy(residual_in.at[:, lanes(hx)], residual, load_sem.at[SL]))
    loads = []
    for n in range(SL):
        here = lanes((2 * x + n) % SL)
        for j, (source, target) in enumerate(((wg_in, wg), (wu_in, wu), (wd_in, wd))):
            loads.append(pltpu.make_async_copy(source.at[:, here], target.at[n], load_sem.at[SL + 1 + 3 * n + j]))
    greet(seq, x, c)
    for copy in front:
        copy.start()
    for copy in loads:
        copy.start()

    mail = Mail(send_sem, recv_sem)
    local_attention(q, k, v, decay, docs, states, head_out, carry)
    carry_states(mail, seq, states, arrived, entering, incoming, lambda: fill_pick(ids, pick))
    attention_rows(head_out, carry, incoming, attn)
    for copy in front:
        copy.wait()
    project(mail, x, c, attn, wo, to_twin, from_twin, part, s1, s2, residual, hidden)
    out = Cross(out_send, out_recv, x, c)
    rows_to_experts(out, x, c, hidden, pick, slot_out, slots)
    norm_rows(x, slots, gain, rows)

    home = Cross(back_send, back_recv, x, c)

    def finish(dx):
        if dx == 0:
            home.send(0, 1 - c, done.at[1 - c], back.at[hx])
            back[hx] = done[c]
        else:
            for to in (0, 1):
                home.send(dx, to, done.at[2 * dx + to], back.at[hx])

    run_experts(mail, seq, rows, p, wg, wu, wd, acc_g, acc_u, act, r1, r2, q1, q2, loads, done, finish)

    weighted = []
    for e in range(SL):
        own = jnp.where(ids[0:1, :] == e, weights[0:1, :], 0.0) + jnp.where(ids[1:2, :] == e, weights[1:2, :], 0.0)
        weighted.append(f32(pick[e]) * own)
    weighted = jnp.concatenate(weighted, axis=0)
    high = bf16(weighted)
    low = bf16(weighted - f32(high))
    home.arrived(0, 1 - c, back.at[2 * x + 1 - c])
    for dx in (3, 1, 2):
        for own in (0, 1):
            home.arrived(dx, own, back.at[2 * ((x + 4 - dx) % 4) + own])
    expert_out = bf16(f32(back[...]).reshape(SL * CAP, W))
    result[...] = bf16(hidden[...] + dot(high, expert_out, 0, 0) + dot(low, expert_out, 0, 0))
    mail.drain()
    out.drain()
    home.drain()


def fill_pick(ids, pick):
    for e, block in enumerate(dispatch(ids)):
        pick[e] = bf16(block)


N_MAIL = 30 + 4 + 6 + 40 + 48 + 12


def shards(queries, keys, values, log_decay, doc_ids, residual, out_weight, norm_gain, expert_ids, route_weight, w_gate, w_up, w_down):
    vmem = pl.BlockSpec(memory_space=pltpu.VMEM)
    hbm = pl.BlockSpec(memory_space=pl.ANY)
    bf, fl = jnp.bfloat16, jnp.float32
    dma = pltpu.SemaphoreType.DMA
    scratch = [
        ((SL, HEADS * HS, W), bf), ((T, W), bf), ((SL, CAP, T), bf),
        ((N_SEQ, 48, HS), bf), ((N_SEQ, 48, HS), bf), ((N_SEQ, 32, HS), bf), ((N_SEQ, 32, HS), bf),
        ((HEADS, T, HS), fl), ((HEADS, T, HS), bf), ((T, HEADS * HS), bf),
        ((4, 2, HALF, W), bf), ((4, 2, HALF, W), bf), ((4, 2, HALF, W), bf), ((2, HALF, W), bf), ((2, 2, HALF, W), bf),
        ((T, W), fl), ((SL, CAP, WS), bf), ((SL, CAP, WS), bf),
        ((16, SL, CAP, W), bf), ((16, SL, CAP, W), bf), ((SL, F, W), bf), ((SL, F, W), bf), ((SL, F, W), bf),
        ((4 * CAP, F), fl), ((4 * CAP, F), fl), ((4 * CAP, F), bf),
        ((2, 4, 2, 2, CAP, W), bf), ((2, 4, 2, 2, 2, CAP, W), bf), ((2, 2, 2, CAP, W), bf), ((2, 2, 2, 2, CAP, W), bf),
        ((SL, CAP, W), bf), ((SL, CAP, W), bf),
    ]
    return pl.pallas_call(
        layer_kernel,
        out_shape=jax.ShapeDtypeStruct((T, W), bf),
        in_specs=[vmem] * 5 + [hbm, hbm] + [vmem] * 3 + [hbm] * 3,
        out_specs=vmem,
        scratch_shapes=[pltpu.VMEM(*s) for s in scratch]
        + [dma((SL + 1 + 3 * SL,)), dma((N_MAIL,)), dma((N_MAIL,)), dma((8,)), dma((8,)), dma((8,)), dma((8,))],
        compiler_params=pltpu.CompilerParams(collective_id=0, has_side_effects=True, vmem_limit_bytes=60 * 2**20),
        name="layer",
    )(queries, keys, values, log_decay.T, doc_ids.reshape(1, T), residual, out_weight, norm_gain.reshape(SL, W),
      expert_ids.T, route_weight.T, w_gate[0].T, w_up[0].T, w_down[0])


def solution(mesh):
    return jax.shard_map(
        shards,
        mesh=mesh,
        in_specs=(
            P("seq", "hx"),
            P("seq", "hx"),
            P("seq", "hx"),
            P("seq", "hx"),
            P("seq"),
            P("seq", None),
            P("hx", None),
            P(),
            P("seq", None),
            P("seq", None),
            P("hx", None, "seq"),
            P("hx", None, "seq"),
            P("hx", "seq", None),
        ),
        out_specs=P("seq", "hx"),
        check_vma=False,
    )
```

```python
import jax
import jax.numpy as jnp
from jax import lax
from jax.experimental import pallas as pl
from jax.experimental.pallas import tpu as pltpu
from jax.sharding import PartitionSpec as P

MESH = pl.DeviceIdType.MESH
CAP = 40
HS = 128
HEADS = 4
T = 128
N_SEQ = 16
SL = 8
W = 768
HW = W // 2
F = 288
ORDER = [(0, 0), (1, 0), (3, 0), (0, 1), (0, 3), (1, 1), (1, 3), (3, 1), (3, 3), (2, 0), (0, 2), (1, 2), (3, 2), (2, 1), (2, 3), (2, 2)]
SLOT = {r: i for i, r in enumerate(ORDER)}


def at(half, first, second):
    return SLOT[(first % 4, second % 4) if half == 0 else (second % 4, first % 4)]


class Mail:
    def __init__(self, send_sem, recv_sem):
        self.send_sem, self.recv_sem = send_sem, recv_sem
        self.number, self.sent = {}, []

    def make(self, key, src, dst, device):
        n = self.number.setdefault(key, len(self.number))
        return pltpu.make_async_remote_copy(
            src_ref=src, dst_ref=dst, send_sem=self.send_sem.at[n], recv_sem=self.recv_sem.at[n],
            device_id=device, device_id_type=MESH)

    def send(self, key, src, dst, device):
        copy = self.make(key, src, dst, device)
        copy.start()
        self.sent.append(copy)

    def arrived(self, key, dst, device):
        self.make(key, dst, dst, device).wait_recv()

    def drain(self):
        for copy in self.sent:
            copy.wait_send()


def ring(half, seq):
    y, z = seq // 4, seq % 4
    yp, ym = ((y + 1) % 4) * 4 + z, ((y + 3) % 4) * 4 + z
    zp, zm = y * 4 + (z + 1) % 4, y * 4 + (z + 3) % 4
    ids = (yp, ym, zp, zm) if half == 0 else (zp, zm, yp, ym)
    return [{"seq": i} for i in ids]


def position(dx, turn):
    return 4 * (dx // 2) + dx % 2 + 2 * turn


class Gather:
    def __init__(self, mail, x, half, turn, seq):
        self.mail, self.x, self.half, self.turn = mail, x, half, turn
        self.fp, self.fm, self.sp, self.sm = ring(half, seq)

    def part(self, f, s, unit):
        lo = 4 * self.half + 2 * self.turn
        return self.x.at[at(self.half, f, s), pl.ds(lo, 2) if unit is None else pl.ds(lo + unit, 1)]

    def push(self, f, s, unit, device, tf, ts):
        key = ("g", self.half, self.turn, tf % 4, ts % 4, unit)
        self.mail.send(key, self.part(f, s, unit), self.part(tf, ts, unit), device)

    def got(self, f, s, unit):
        self.mail.arrived(("g", self.half, self.turn, f % 4, s % 4, unit), self.part(f, s, unit), self.fp)

    def across(self, f):
        self.push(f, 0, None, self.sp, f, 3)
        self.push(f, 0, None, self.sm, f, 1)

    def start(self):
        self.push(0, 0, None, self.fp, 3, 0)
        self.push(0, 0, None, self.fm, 1, 0)
        self.across(0)

    def first(self, f):
        self.got(f, 0, None)
        if f == 3:
            self.push(3, 0, 0, self.fp, 2, 0)
        else:
            self.push(1, 0, 1, self.fm, 2, 0)
        self.across(f)

    def first_far(self):
        self.got(2, 0, 0)
        self.got(2, 0, 1)
        self.across(2)

    def second(self, f):
        self.got(f, 3, None)
        self.push(f, 3, 0, self.sp, f, 2)
        self.got(f, 1, None)
        self.push(f, 1, 1, self.sm, f, 2)

    def second_far(self, f):
        self.got(f, 2, 0)
        self.got(f, 2, 1)


class Reduce:
    def __init__(self, mail, p, r1, r2, q1, q2, half, turn, seq):
        self.mail, self.p, self.half, self.turn = mail, p, half, turn
        self.r1, self.r2, self.q1, self.q2 = r1.at[half, turn], r2.at[half, turn], q1.at[half, turn], q2.at[half, turn]
        self.fp, self.fm, self.sp, self.sm = ring(half, seq)

    def unit(self, f, s, u):
        return self.p.at[at(self.half, f, s), 4 * self.half + 2 * self.turn + u]

    def push(self, key, src, dst, device):
        self.mail.send((self.half, self.turn) + key, src, dst, device)

    def got(self, key, dst):
        self.mail.arrived((self.half, self.turn) + key, dst, self.fp)
        return dst

    def total(self, f, s, u, *others):
        total = f32(self.unit(f, s, u)[...])
        for other in others:
            total += f32(other[...])
        return bf16(total)

    def add(self, f, s, u, *others):
        self.unit(f, s, u)[...] = self.total(f, s, u, *others)

    def start(self, f):
        self.push(("r1", f, 0), self.unit(f, 2, 0), self.r1.at[f, 0], self.sp)
        self.push(("r1", f, 1), self.unit(f, 2, 1), self.r1.at[f, 1], self.sm)
        self.push(("r2", f, 0, 1), self.unit(f, 1, 1), self.r2.at[f, 0, 1], self.sp)
        self.push(("r2", f, 1, 0), self.unit(f, 3, 0), self.r2.at[f, 1, 0], self.sm)

    def middle(self, f):
        self.add(f, 1, 0, self.got(("r1", f, 0), self.r1.at[f, 0]))
        self.push(("r2", f, 0, 0), self.unit(f, 1, 0), self.r2.at[f, 0, 0], self.sp)
        self.add(f, 3, 1, self.got(("r1", f, 1), self.r1.at[f, 1]))
        self.push(("r2", f, 1, 1), self.unit(f, 3, 1), self.r2.at[f, 1, 1], self.sm)

    def end(self, f):
        for u in (1, 0) if f == 1 else (0, 1):
            self.add(f, 0, u, self.got(("r2", f, 0, u), self.r2.at[f, 0, u]),
                     self.got(("r2", f, 1, u), self.r2.at[f, 1, u]))
            if f == 2:
                self.push(("q1", u), self.unit(2, 0, u), self.q1.at[u], (self.fp, self.fm)[u])
            if f == 1:
                if u == 0:
                    self.add(1, 0, 0, self.got(("q1", 0), self.q1.at[0]))
                self.push(("q2", 0, u), self.unit(1, 0, u), self.q2.at[0, u], self.fp)
            if f == 3:
                if u == 1:
                    self.add(3, 0, 1, self.got(("q1", 1), self.q1.at[1]))
                self.push(("q2", 1, u), self.unit(3, 0, u), self.q2.at[1, u], self.fm)

    def last(self, u, out):
        a = self.got(("q2", 0, u), self.q2.at[0, u])
        b = self.got(("q2", 1, u), self.q2.at[1, u])
        out[4 * self.half + 2 * self.turn + u] = self.total(0, 0, u, a, b)


def iota(shape, dim):
    return lax.broadcasted_iota(jnp.int32, shape, dim)


def lanes(n):
    return pl.ds(pl.multiple_of(n * W, W), W)


def f32(a):
    return a.astype(jnp.float32)


def bf16(a):
    return a.astype(jnp.bfloat16)


def dot(a, b, ca=1, cb=0, **kw):
    return lax.dot_general(a, b, (((ca,), (cb,)), ((), ())), preferred_element_type=jnp.float32, **kw)


def dispatch(ids):
    experts = iota((SL, T), 0)
    named = (ids[0:1, :] == experts) | (ids[1:2, :] == experts)
    before = bf16(jnp.where(iota((T, T), 0) < iota((T, T), 1), 1.0, 0.0))
    rank = dot(bf16(jnp.where(named, 1.0, 0.0)), before)
    slot = f32(iota((CAP, T), 0))
    chosen = f32(jnp.where(named, 1.0, 0.0))
    return [jnp.where(rank[e : e + 1, :] == slot, 1.0, 0.0) * chosen[e : e + 1, :] for e in range(SL)]


def greet(seq, x, c):
    others = [{"seq": (seq + d) % N_SEQ} for d in range(1, N_SEQ)]
    others += [{"hx": (2 * x + c + d) % SL} for d in range(1, SL)]
    barrier = pltpu.get_barrier_semaphore()
    for device in others:
        pl.semaphore_signal(barrier, inc=1, device_id=device, device_id_type=MESH)
    return lambda: pl.semaphore_wait(barrier, len(others))


def local_attention(q, k, v, decay, docs, states, head_out, carry):
    doc_row = jnp.broadcast_to(f32(docs[...]), (T, T))
    doc_col = doc_row.T
    allowed = (iota((T, T), 0) >= iota((T, T), 1)) & (doc_row == doc_col)
    upto = f32(jnp.where(iota((T, T), 0) <= iota((T, T), 1), 1.0, 0.0))
    rows = jnp.concatenate([decay[...], jnp.zeros((8 - HEADS, T), jnp.float32)], axis=0)
    sums = dot(rows, upto, precision=lax.Precision.HIGHEST)
    first, last = doc_col[0:1, :], doc_col[T - 1 : T, :]
    row = iota((16, HS), 0)
    for h in range(HEADS):
        lanes = slice(h * HS, (h + 1) * HS)
        across = jnp.broadcast_to(sums[h : h + 1, :], (T, T))
        down = across.T
        fade = jnp.where(allowed, jnp.exp(jnp.where(allowed, down - across, 0.0)), 0.0)
        scores = dot(q[:, lanes], k[:, lanes], 1, 1)
        head_out[h] = dot(bf16(scores * fade), v[:, lanes])
        total = down[T - 1 : T, :]
        to_end = jnp.where(doc_col == last, jnp.exp(total - down), 0.0)
        state = bf16(dot(bf16(f32(k[:, lanes]) * to_end), v[:, lanes], 0, 0))
        carry[h] = bf16(f32(q[:, lanes]) * jnp.where(doc_col == first, jnp.exp(down), 0.0))
        high = f32(bf16(total))
        mid = f32(bf16(total - high))
        low = total - high - mid
        facts = jnp.where(row == 0, high, jnp.where(row == 1, mid, jnp.where(row == 2, low, jnp.where(row == 3, first, last))))
        for part in range(4):
            states[4 * h + part, 0:32] = state[32 * part : 32 * (part + 1)]
            states[4 * h + part, 32:48] = bf16(facts)


def carry_states(mail, seq, states, arrived, entering, incoming):
    for d in range(1, N_SEQ):
        mail.send(("s", d), states.at[(seq + d) % N_SEQ], arrived.at[seq], {"seq": (seq + d) % N_SEQ})
    arrived[seq] = states[seq]
    for d in range(1, N_SEQ):
        mail.arrived(("s", d), arrived.at[(seq + N_SEQ - d) % N_SEQ], {"seq": (seq + d) % N_SEQ})
    state = jnp.zeros((32, HS), jnp.float32)
    before = jnp.full((1, HS), -1.0, jnp.float32)
    for s in range(N_SEQ):
        facts = f32(arrived[s, 32:48])
        log_total = facts[0:1] + facts[1:2] + facts[2:3]
        first, last = facts[3:4], facts[4:5]
        state = state * jnp.where(before == first, 1.0, 0.0)
        entering[s] = bf16(state)
        state = state * jnp.where(first == last, jnp.exp(log_total), 0.0) + f32(arrived[s, 0:32])
        before = last
    for d in range(1, N_SEQ):
        mail.send(("c", d), entering.at[(seq + d) % N_SEQ], incoming.at[seq], {"seq": (seq + d) % N_SEQ})
    incoming[seq] = entering[seq]
    for d in range(1, N_SEQ):
        mail.arrived(("c", d), incoming.at[(seq + N_SEQ - d) % N_SEQ], {"seq": (seq + d) % N_SEQ})


def attention_rows(head_out, carry, incoming, attn):
    for h in range(HEADS):
        state = incoming[4 * h : 4 * h + 4].reshape(HS, HS)
        out = head_out[h] + dot(carry[h], state)
        mean = jnp.mean(out * out, axis=1, keepdims=True)
        attn[:, h * HS : (h + 1) * HS] = bf16(out * lax.rsqrt(mean + 1e-05))


HALF = T // 2


class Project:
    def __init__(self, mail, x, c, turn, attn, wo, to_twin, from_twin, part, r1, r2, residual, hidden):
        self.mail, self.c, self.turn, self.attn, self.wo = mail, c, turn, attn, wo
        self.to_twin, self.from_twin, self.part = to_twin.at[turn], from_twin.at[turn], part.at[turn]
        self.r1, self.r2, self.residual, self.hidden = r1.at[turn], r2.at[turn], residual, hidden
        self.twin = {"hx": 2 * x + 1 - c}
        self.up, self.down = {"hx": 2 * ((x + 1) % 4) + c}, {"hx": 2 * ((x + 3) % 4) + c}
        self.lanes = slice(turn * HW, (turn + 1) * HW)

    def product(self, n):
        return dot(self.attn[...], self.wo[n, :, self.lanes]).reshape(2, HALF, HW)

    def send(self, key, src, dst, device):
        self.mail.send((self.turn,) + key, src, dst, device)

    def got(self, key, dst):
        self.mail.arrived((self.turn,) + key, dst, self.up)
        return f32(dst[...])

    def start(self):
        for dx in (2, 1, 3, 0):
            self.to_twin[dx] = bf16(self.product(2 * dx + 1 - self.c))
            self.send(("t", dx), self.to_twin.at[dx], self.from_twin.at[dx], self.twin)

    def both(self, dx):
        return self.product(2 * dx + self.c) + self.got(("t", dx), self.from_twin.at[dx])

    def away(self):
        part = self.part
        part[2] = bf16(self.both(2))
        self.send(("p1", 0), part.at[2, 0], self.r1.at[0], self.up)
        self.send(("p1", 1), part.at[2, 1], self.r1.at[1], self.down)
        mine = self.both(1)
        part[1, 1] = bf16(mine[1])
        self.send(("p2", 0, 1), part.at[1, 1], self.r2.at[0, 1], self.up)
        self.mine_up = mine[0]
        mine = self.both(3)
        part[3, 0] = bf16(mine[0])
        self.send(("p2", 1, 0), part.at[3, 0], self.r2.at[1, 0], self.down)
        self.mine_down = mine[1]
        self.mine = self.both(0)

    def onward(self):
        self.part[1, 0] = bf16(self.mine_up + self.got(("p1", 0), self.r1.at[0]))
        self.send(("p2", 0, 0), self.part.at[1, 0], self.r2.at[0, 0], self.up)
        self.part[3, 1] = bf16(self.mine_down + self.got(("p1", 1), self.r1.at[1]))
        self.send(("p2", 1, 1), self.part.at[3, 1], self.r2.at[1, 1], self.down)

    def home(self):
        for u in (1, 0):
            rows = slice(u * HALF, (u + 1) * HALF)
            total = f32(self.residual[rows, self.lanes]) + self.mine[u]
            total += self.got(("p2", 0, u), self.r2.at[0, u])
            total += self.got(("p2", 1, u), self.r2.at[1, u])
            self.hidden[rows, self.lanes] = total


class Cross:
    def __init__(self, send_sem, recv_sem, number, x, c):
        self.send_sem, self.recv_sem, self.base, self.x, self.c, self.sent = send_sem, recv_sem, 8 * number, x, c, []

    def make(self, dx, to, own, src, dst):
        return pltpu.make_async_remote_copy(
            src_ref=src, dst_ref=dst, send_sem=self.send_sem.at[self.base + 2 * dx + to],
            recv_sem=self.recv_sem.at[self.base + 2 * dx + own], device_id={"hx": 2 * ((self.x + dx) % 4) + to}, device_id_type=MESH)

    def send(self, dx, to, src, dst):
        copy = self.make(dx, to, self.c, src, dst)
        copy.start()
        self.sent.append(copy)

    def arrived(self, dx, own, dst):
        self.make(dx, own, own, dst, dst).wait_recv()

    def drain(self):
        for copy in self.sent:
            copy.wait_send()


def rows_to_experts(cross, facts, x, c, turn, hidden, gain, pick, out, facts_out, block, facts_in):
    hx = 2 * x + c
    own = pl.ds(pl.multiple_of(hx * W + turn * HW, 128), HW)
    rows = bf16(hidden[:, turn * HW : (turn + 1) * HW] * gain[:, own])
    if turn == 1:
        square = jnp.sum(hidden[...] * hidden[...], axis=1, keepdims=True)
        high = f32(bf16(square))
        rows = jnp.concatenate([rows, bf16(jnp.where(iota((T, 128), 1) < 64, high, square - high))], axis=1)
    for dx, to in ((2, 0), (2, 1), (1, 0), (1, 1), (3, 0), (3, 1), (0, 1 - c)):
        n = 2 * dx + (to if dx else 0)
        slots = bf16(dot(pick[2 * ((x + dx) % 4) + to], rows))
        if turn == 1:
            facts_out[n] = slots[:, HW:]
            facts.send(dx, to, facts_out.at[n], facts_in.at[2 * ((4 - dx) % 4) + c])
        out[turn, n] = slots[:, :HW]
        cross.send(dx, to, out.at[turn, n], block.at[position((4 - dx) % 4, turn), c])
    slots = bf16(dot(pick[hx], rows))
    block[position(0, turn), c] = slots[:, :HW]
    if turn == 1:
        facts_in[c] = slots[:, HW:]


def from_row(cross, c, place):
    cross.arrived(0, 1 - c, place(0, 1 - c))
    for dx in (1, 3, 2):
        for own in (0, 1):
            cross.arrived(dx, own, place(4 - dx, own))


def send_scale(mail, seq, facts_in, scale_out, scales):
    square = sum(f32(facts_in[k]) for k in range(SL))
    mean = (square[:, 0:1] + square[:, 64:65]) * (1.0 / (SL * W))
    scale = lax.rsqrt(mean + 1e-06)
    row = jnp.sum(jnp.where(iota((CAP, 128), 0) == iota((CAP, 128), 1), scale, 0.0), axis=0, keepdims=True)
    scale_out[...] = jnp.broadcast_to(row, (8, 128))
    scales[0] = jnp.broadcast_to(row, (8, 128))
    for dy, dz in ORDER[1:]:
        device = {"seq": ((seq // 4 + dy) % 4) * 4 + (seq % 4 + dz) % 4}
        place = SLOT[((4 - dy) % 4, (4 - dz) % 4)]
        mail.send(("n", place), scale_out, scales.at[place], device)


def scale_column(scales, group):
    own = iota((CAP, 128), 0) == iota((CAP, 128), 1)
    return jnp.concatenate(
        [jnp.sum(jnp.where(own, scales[4 * group + b, 0:1, :], 0.0), axis=1, keepdims=True) for b in range(4)], axis=0)


def run_experts(mail, seq, rows, p, wgu, wd, acc, act, scales, r1, r2, q1, q2, loads, out, first_rows, second_rows, finish, combine):
    gathers = [[Gather(mail, rows, half, turn, seq) for half in (0, 1)] for turn in (0, 1)]
    reduces = [[Reduce(mail, p, r1, r2, q1, q2, half, turn, seq) for half in (0, 1)] for turn in (0, 1)]

    def up(group, turn):
        blocks = slice(4 * group, 4 * group + 4)
        parts = [rows[blocks, position(n // 2, turn), n % 2].reshape(4 * CAP, HW) for n in range(SL)]
        block = jnp.concatenate(parts, axis=1)
        total = dot(block, wgu[turn], 1, 1)
        if turn == 0:
            acc[group] = total
        else:
            total = (total + acc[group]) * scale_column(scales, group)
            gate = total[:, 0:F]
            act[group] = bf16(gate / (1.0 + jnp.exp(-gate)) * total[:, F : 2 * F])

    def down(group, turn):
        blocks = slice(4 * group, 4 * group + 4)
        for dx in range(4):
            block = dot(act[group], wd[turn, :, dx * W : (dx + 1) * W])
            for core in (0, 1):
                half = block[:, core * HW : (core + 1) * HW]
                p[blocks, position(dx, turn), core] = bf16(half.reshape(4, CAP, HW))

    def each(step, turn, *args, of=gathers):
        for one in of[turn]:
            getattr(one, step)(*args)

    def reduce(turn, *steps):
        for step in steps:
            each({"s": "start", "m": "middle", "e": "end"}[step[0]], turn, int(step[1]), of=reduces)

    def end(turn):
        for u in (1, 0):
            for half in (1, 0):
                reduces[turn][half].last(u, out)
                finish(2 * half + u, turn)

    first_rows()
    each("start", 0)
    second_rows()
    each("first", 0, 3)
    each("first", 0, 1)
    each("second", 0, 0)
    each("first_far", 0)
    second_rows(True)
    each("start", 1)
    each("second", 0, 3)
    each("second", 0, 1)
    for copy in loads:
        copy.wait()
    up(0, 0)
    each("first", 1, 3)
    each("first", 1, 1)
    each("second", 0, 2)
    each("second", 1, 0)
    up(1, 0)
    for f in (0, 3, 1):
        each("second_far", 0, f)
    each("first_far", 1)
    up(2, 0)
    each("second", 1, 3)
    each("second", 1, 1)
    each("second_far", 0, 2)
    up(3, 0)
    for place in range(1, N_SEQ):
        mail.arrived(("n", place), scales.at[place], {"seq": (seq + 1) % N_SEQ})
    up(0, 1)
    down(0, 0)
    each("second", 1, 2)
    up(1, 1)
    down(1, 0)
    for f in (0, 3, 1):
        each("second_far", 1, f)
    up(2, 1)
    down(2, 0)
    each("second_far", 1, 2)
    up(3, 1)
    down(3, 0)

    reduce(0, "s2", "s1")
    down(0, 1)
    reduce(0, "m2", "s3")
    down(1, 1)
    reduce(0, "m1", "e2", "s0")
    down(2, 1)
    down(3, 1)
    reduce(0, "m3")
    reduce(1, "s2")
    reduce(0, "e1", "m0")
    reduce(1, "s1")
    reduce(0, "e3")
    reduce(1, "m2")
    reduce(0, "e0")
    reduce(1, "s3", "m1")
    end(0)
    reduce(1, "e2", "s0", "m3", "e1", "m0", "e3", "e0")
    combine(0)
    end(1)
    combine(1)


def layer_kernel(q, k, v, decay, docs, residual_in, wo_in, gain, ids, weights, wg_in, wu_in, wd_in, result,
                 wo, residual, pick, states, arrived, entering, incoming, head_out, carry, attn,
                 to_twin, from_twin, part, s1, s2, hidden, slot_out, facts_out, facts_in, scale_out, scales,
                 rows, p, wgu, wd, acc, act, r1, r2, q1, q2, done, back,
                 load_sem, send_sem, recv_sem, cross_send, cross_recv):
    seq, hx = lax.axis_index("seq"), lax.axis_index("hx")
    x, c = hx // 2, hx % 2

    arrive = greet(seq, x, c)
    front, loads = [], []

    def load(copies, source, target):
        n = len(front) + len(loads)
        copies.append(pltpu.make_async_copy(source, target, load_sem.at[n]))
        copies[-1].start()

    for n in range(SL):
        load(front, wo_in.at[:, lanes(2 * ((x + n // 2) % 4) + n % 2)], wo.at[n])
    load(front, residual_in.at[:, lanes(hx)], residual)
    for turn in (0, 1):
        for n in range(SL):
            slice_at = (2 * ((x + n // 2) % 4) + n % 2) * W + turn * HW
            here, target = pl.ds(pl.multiple_of(slice_at, 128), HW), slice(n * HW, (n + 1) * HW)
            load(loads, wg_in.at[:, here], wgu.at[turn, 0:F, target])
            load(loads, wu_in.at[:, here], wgu.at[turn, F : 2 * F, target])
            load(loads, wd_in.at[:, here], wd.at[turn, :, target])

    mail = Mail(send_sem, recv_sem)
    local_attention(q, k, v, decay, docs, states, head_out, carry)
    fill_pick(ids, pick)
    arrive()
    carry_states(mail, seq, states, arrived, entering, incoming)
    attention_rows(head_out, carry, incoming, attn)
    for copy in front:
        copy.wait()
    projects = [Project(mail, x, c, turn, attn, wo, to_twin, from_twin, part, s1, s2, residual, hidden) for turn in (0, 1)]
    crosses = [Cross(cross_send, cross_recv, number, x, c) for number in range(5)]
    own = rows.at[0]

    def dispatch(turn):
        rows_to_experts(crosses[turn], crosses[2], x, c, turn, hidden, gain, pick, slot_out, facts_out, own, facts_in)

    def first_rows():
        projects[0].start()
        projects[0].away()
        projects[1].start()
        projects[0].onward()
        projects[1].away()
        projects[0].home()
        dispatch(0)
        projects[1].onward()
        from_row(crosses[0], c, lambda dx, core: own.at[position(dx, 0), core])

    def second_rows(here=False):
        if here:
            from_row(crosses[2], c, lambda dx, core: facts_in.at[2 * dx + core])
            send_scale(mail, seq, facts_in, scale_out, scales)
            from_row(crosses[1], c, lambda dx, core: own.at[position(dx, 1), core])
        else:
            projects[1].home()
            dispatch(1)

    def finish(dx, turn):
        for to in (0, 1) if dx else (1 - c,):
            crosses[3 + turn].send(dx, to, done.at[position(dx, turn), to], back.at[turn, hx])
        if dx == 0:
            back[turn, hx] = done[position(0, turn), c]

    def combine(turn):
        weighted = []
        for e in range(SL):
            share = jnp.where(ids[0:1, :] == e, weights[0:1, :], 0.0) + jnp.where(ids[1:2, :] == e, weights[1:2, :], 0.0)
            weighted.append(f32(pick[e]) * share)
        weighted = jnp.concatenate(weighted, axis=0)
        high = bf16(weighted)
        low = bf16(weighted - f32(high))
        from_row(crosses[3 + turn], c, lambda dx, core: back.at[turn, 2 * ((x + dx) % 4) + core])
        expert_out = bf16(f32(back[turn]).reshape(SL * CAP, HW))
        half = slice(turn * HW, (turn + 1) * HW)
        result[:, half] = bf16(hidden[:, half] + dot(high, expert_out, 0, 0) + dot(low, expert_out, 0, 0))

    run_experts(mail, seq, rows, p, wgu, wd, acc, act, scales, r1, r2, q1, q2, loads, done,
                first_rows, second_rows, finish, combine)
    mail.drain()
    for cross in crosses:
        cross.drain()


def fill_pick(ids, pick):
    for e, block in enumerate(dispatch(ids)):
        pick[e] = bf16(block)


N_MAIL = 30 + 15 + 2 * (4 + 6 + 40 + 48 + 12)


def shards(queries, keys, values, log_decay, doc_ids, residual, out_weight, norm_gain, expert_ids, route_weight, w_gate, w_up, w_down):
    vmem = pl.BlockSpec(memory_space=pltpu.VMEM)
    hbm = pl.BlockSpec(memory_space=pl.ANY)
    bf, fl = jnp.bfloat16, jnp.float32
    dma = pltpu.SemaphoreType.DMA
    unit = (2, CAP, HW)
    scratch = [
        ((SL, HEADS * HS, W), bf), ((T, W), bf), ((SL, CAP, T), bf),
        ((N_SEQ, 48, HS), bf), ((N_SEQ, 48, HS), bf), ((N_SEQ, 32, HS), bf), ((N_SEQ, 32, HS), bf),
        ((HEADS, T, HS), fl), ((HEADS, T, HS), bf), ((T, HEADS * HS), bf),
        ((2, 4, 2, HALF, HW), bf), ((2, 4, 2, HALF, HW), bf), ((2, 4, 2, HALF, HW), bf),
        ((2, 2, HALF, HW), bf), ((2, 2, 2, HALF, HW), bf),
        ((T, W), fl), ((2, SL, CAP, HW), bf), ((SL, CAP, 128), bf), ((SL, CAP, 128), bf), ((8, 128), fl), ((16, 8, 128), fl),
        ((16, SL) + unit, bf), ((16, SL) + unit, bf), ((2, 2 * F, 4 * W), bf), ((2, F, 4 * W), bf),
        ((4, 4 * CAP, 2 * F), fl), ((4, 4 * CAP, F), bf),
        ((2, 2, 4, 2) + unit, bf), ((2, 2, 4, 2, 2) + unit, bf), ((2, 2, 2) + unit, bf), ((2, 2, 2, 2) + unit, bf),
        ((SL,) + unit, bf), ((2, SL, CAP, HW), bf),
    ]
    return pl.pallas_call(
        layer_kernel,
        out_shape=jax.ShapeDtypeStruct((T, W), bf),
        in_specs=[vmem] * 5 + [hbm, hbm] + [vmem] * 3 + [hbm] * 3,
        out_specs=vmem,
        scratch_shapes=[pltpu.VMEM(*s) for s in scratch]
        + [dma((SL + 1 + 6 * SL,)), dma((N_MAIL,)), dma((N_MAIL,)), dma((40,)), dma((40,))],
        compiler_params=pltpu.CompilerParams(collective_id=0, has_side_effects=True, vmem_limit_bytes=60 * 2**20),
        name="layer",
    )(queries, keys, values, log_decay.T, doc_ids.reshape(1, T), residual, out_weight, norm_gain.reshape(1, SL * W),
      expert_ids.T, route_weight.T, w_gate[0].T, w_up[0].T, w_down[0])


def solution(mesh):
    return jax.shard_map(
        shards,
        mesh=mesh,
        in_specs=(
            P("seq", "hx"),
            P("seq", "hx"),
            P("seq", "hx"),
            P("seq", "hx"),
            P("seq"),
            P("seq", None),
            P("hx", None),
            P(),
            P("seq", None),
            P("seq", None),
            P("hx", None, "seq"),
            P("hx", None, "seq"),
            P("hx", "seq", None),
        ),
        out_specs=P("seq", "hx"),
        check_vma=False,
    )
```

```python
import jax
import jax.numpy as jnp
from jax import lax
from jax.experimental import pallas as pl
from jax.experimental.pallas import tpu as pltpu
from jax.sharding import PartitionSpec as P

MESH = pl.DeviceIdType.MESH
CAP = 40
HS = 128
HEADS = 4
T = 128
N_SEQ = 16
SL = 8
W = 768
HW = W // 2
F = 288
ORDER = [(0, 0), (1, 0), (3, 0), (0, 1), (0, 3), (1, 1), (1, 3), (3, 1), (3, 3), (2, 0), (0, 2), (3, 2), (1, 2), (2, 3), (2, 1), (2, 2)]
SLOT = {r: i for i, r in enumerate(ORDER)}


def at(half, first, second):
    return SLOT[(first % 4, second % 4) if half == 0 else (second % 4, first % 4)]


def across_plane(seq, dy, dz):
    return (seq // 4 + dy) % 4 * 4 + (seq % 4 + dz) % 4


FAR_FIRST = sorted(ORDER[1:], key=lambda r: -(min(r[0], 4 - r[0]) + min(r[1], 4 - r[1])))


class Mail:
    def __init__(self, send_sem, recv_sem):
        self.send_sem, self.recv_sem = send_sem, recv_sem
        self.number, self.sent = {}, []

    def make(self, key, src, dst, device):
        n = self.number.setdefault(key, len(self.number))
        return pltpu.make_async_remote_copy(
            src_ref=src, dst_ref=dst, send_sem=self.send_sem.at[n], recv_sem=self.recv_sem.at[n],
            device_id=device, device_id_type=MESH)

    def send(self, key, src, dst, device):
        copy = self.make(key, src, dst, device)
        copy.start()
        self.sent.append(copy)

    def arrived(self, key, dst, device):
        self.make(key, dst, dst, device).wait_recv()

    def drain(self):
        for copy in self.sent:
            copy.wait_send()


def ring(half, seq):
    y, z = seq // 4, seq % 4
    yp, ym = ((y + 1) % 4) * 4 + z, ((y + 3) % 4) * 4 + z
    zp, zm = y * 4 + (z + 1) % 4, y * 4 + (z + 3) % 4
    ids = (yp, ym, zp, zm) if half == 0 else (zp, zm, yp, ym)
    return [{"seq": i} for i in ids]


def position(dx, turn):
    return 4 * (dx // 2) + dx % 2 + 2 * turn


class Gather:
    def __init__(self, mail, x, half, turn, seq):
        self.mail, self.x, self.half, self.turn = mail, x, half, turn
        self.fp, self.fm, self.sp, self.sm = ring(half, seq)

    def part(self, f, s, unit):
        lo = 4 * self.half + 2 * self.turn
        return self.x.at[at(self.half, f, s), pl.ds(lo, 2) if unit is None else pl.ds(lo + unit, 1)]

    def push(self, f, s, unit, device, tf, ts):
        key = ("g", self.half, self.turn, tf % 4, ts % 4, unit)
        self.mail.send(key, self.part(f, s, unit), self.part(tf, ts, unit), device)

    def got(self, f, s, unit):
        self.mail.arrived(("g", self.half, self.turn, f % 4, s % 4, unit), self.part(f, s, unit), self.fp)

    def across(self, f):
        self.push(f, 0, None, self.sp, f, 3)
        self.push(f, 0, None, self.sm, f, 1)

    def start(self):
        self.push(0, 0, None, self.fp, 3, 0)
        self.push(0, 0, None, self.fm, 1, 0)
        self.across(0)

    def first(self, f):
        self.got(f, 0, None)
        if f == 3:
            self.push(3, 0, 0, self.fp, 2, 0)
        else:
            self.push(1, 0, 1, self.fm, 2, 0)
        self.across(f)

    def first_far(self):
        self.got(2, 0, 0)
        self.got(2, 0, 1)
        self.across(2)

    def second(self, f):
        self.got(f, 3, None)
        self.push(f, 3, 0, self.sp, f, 2)
        self.got(f, 1, None)
        self.push(f, 1, 1, self.sm, f, 2)

    def second_far(self, f):
        self.got(f, 2, 0)
        self.got(f, 2, 1)


class Reduce:
    def __init__(self, mail, p, r1, r2, q1, q2, half, turn, seq):
        self.mail, self.p, self.half, self.turn = mail, p, half, turn
        self.r1, self.r2, self.q1, self.q2 = r1.at[half, turn], r2.at[half, turn], q1.at[half, turn], q2.at[half, turn]
        self.fp, self.fm, self.sp, self.sm = ring(half, seq)

    def unit(self, f, s, u):
        return self.p.at[at(self.half, f, s), 4 * self.half + 2 * self.turn + u]

    def push(self, key, src, dst, device):
        self.mail.send((self.half, self.turn) + key, src, dst, device)

    def got(self, key, dst):
        self.mail.arrived((self.half, self.turn) + key, dst, self.fp)
        return dst

    def total(self, f, s, u, *others):
        total = f32(self.unit(f, s, u)[...])
        for other in others:
            total += f32(other[...])
        return bf16(total)

    def add(self, f, s, u, *others):
        self.unit(f, s, u)[...] = self.total(f, s, u, *others)

    def start(self, f):
        self.push(("r1", f, 0), self.unit(f, 2, 0), self.r1.at[f, 0], self.sp)
        self.push(("r1", f, 1), self.unit(f, 2, 1), self.r1.at[f, 1], self.sm)
        self.push(("r2", f, 0, 1), self.unit(f, 1, 1), self.r2.at[f, 0, 1], self.sp)
        self.push(("r2", f, 1, 0), self.unit(f, 3, 0), self.r2.at[f, 1, 0], self.sm)

    def middle(self, f):
        self.add(f, 1, 0, self.got(("r1", f, 0), self.r1.at[f, 0]))
        self.push(("r2", f, 0, 0), self.unit(f, 1, 0), self.r2.at[f, 0, 0], self.sp)
        self.add(f, 3, 1, self.got(("r1", f, 1), self.r1.at[f, 1]))
        self.push(("r2", f, 1, 1), self.unit(f, 3, 1), self.r2.at[f, 1, 1], self.sm)

    def end(self, f):
        for u in (1, 0) if f == 1 else (0, 1):
            self.add(f, 0, u, self.got(("r2", f, 0, u), self.r2.at[f, 0, u]),
                     self.got(("r2", f, 1, u), self.r2.at[f, 1, u]))
            if f == 2:
                self.push(("q1", u), self.unit(2, 0, u), self.q1.at[u], (self.fp, self.fm)[u])
            if f == 1:
                if u == 0:
                    self.add(1, 0, 0, self.got(("q1", 0), self.q1.at[0]))
                self.push(("q2", 0, u), self.unit(1, 0, u), self.q2.at[0, u], self.fp)
            if f == 3:
                if u == 1:
                    self.add(3, 0, 1, self.got(("q1", 1), self.q1.at[1]))
                self.push(("q2", 1, u), self.unit(3, 0, u), self.q2.at[1, u], self.fm)

    def last(self, u, out):
        a = self.got(("q2", 0, u), self.q2.at[0, u])
        b = self.got(("q2", 1, u), self.q2.at[1, u])
        out[4 * self.half + 2 * self.turn + u] = self.total(0, 0, u, a, b)


def iota(shape, dim):
    return lax.broadcasted_iota(jnp.int32, shape, dim)


def lanes(n):
    return pl.ds(pl.multiple_of(n * W, W), W)


def f32(a):
    return a.astype(jnp.float32)


def bf16(a):
    return a.astype(jnp.bfloat16)


def dot(a, b, ca=1, cb=0, **kw):
    return lax.dot_general(a, b, (((ca,), (cb,)), ((), ())), preferred_element_type=jnp.float32, **kw)


def dispatch(ids):
    experts = iota((SL, T), 0)
    named = (ids[0:1, :] == experts) | (ids[1:2, :] == experts)
    before = bf16(jnp.where(iota((T, T), 0) < iota((T, T), 1), 1.0, 0.0))
    rank = dot(bf16(jnp.where(named, 1.0, 0.0)), before)
    slot = f32(iota((CAP, T), 0))
    chosen = f32(jnp.where(named, 1.0, 0.0))
    return [jnp.where(rank[e : e + 1, :] == slot, 1.0, 0.0) * chosen[e : e + 1, :] for e in range(SL)]


def greet(seq, x, c):
    others = [{"seq": across_plane(seq, *r)} for r in FAR_FIRST]
    others += [{"hx": (2 * x + c + d) % SL} for d in range(1, SL)]
    barrier = pltpu.get_barrier_semaphore()
    for device in others:
        pl.semaphore_signal(barrier, inc=1, device_id=device, device_id_type=MESH)
    return lambda: pl.semaphore_wait(barrier, len(others))


def local_attention(q, k, v, decay, docs, states, head_out, carry):
    doc_row = jnp.broadcast_to(f32(docs[...]), (T, T))
    doc_col = doc_row.T
    allowed = (iota((T, T), 0) >= iota((T, T), 1)) & (doc_row == doc_col)
    upto = f32(jnp.where(iota((T, T), 0) <= iota((T, T), 1), 1.0, 0.0))
    rows = jnp.concatenate([decay[...], jnp.zeros((8 - HEADS, T), jnp.float32)], axis=0)
    sums = dot(rows, upto, precision=lax.Precision.HIGHEST)
    first, last = doc_col[0:1, :], doc_col[T - 1 : T, :]
    row = iota((16, HS), 0)
    for h in range(HEADS):
        lanes = slice(h * HS, (h + 1) * HS)
        across = jnp.broadcast_to(sums[h : h + 1, :], (T, T))
        down = across.T
        fade = jnp.where(allowed, jnp.exp(jnp.where(allowed, down - across, 0.0)), 0.0)
        scores = dot(q[:, lanes], k[:, lanes], 1, 1)
        head_out[h] = dot(bf16(scores * fade), v[:, lanes])
        total = down[T - 1 : T, :]
        to_end = jnp.where(doc_col == last, jnp.exp(total - down), 0.0)
        state = bf16(dot(bf16(f32(k[:, lanes]) * to_end), v[:, lanes], 0, 0))
        carry[h] = bf16(f32(q[:, lanes]) * jnp.where(doc_col == first, jnp.exp(down), 0.0))
        high = f32(bf16(total))
        mid = f32(bf16(total - high))
        low = total - high - mid
        facts = jnp.where(row == 0, high, jnp.where(row == 1, mid, jnp.where(row == 2, low, jnp.where(row == 3, first, last))))
        for part in range(4):
            states[4 * h + part, 0:32] = state[32 * part : 32 * (part + 1)]
            states[4 * h + part, 32:48] = bf16(facts)


def carry_states(mail, seq, states, arrived, entering, incoming):
    for r in FAR_FIRST:
        to = across_plane(seq, *r)
        mail.send(("s", r), states.at[to], arrived.at[seq], {"seq": to})
    arrived[seq] = states[seq]
    for r in reversed(FAR_FIRST):
        mail.arrived(("s", r), arrived.at[across_plane(seq, 4 - r[0], 4 - r[1])], {"seq": across_plane(seq, *r)})
    state = jnp.zeros((32, HS), jnp.float32)
    before = jnp.full((1, HS), -1.0, jnp.float32)
    for s in range(N_SEQ):
        facts = f32(arrived[s, 32:48])
        log_total = facts[0:1] + facts[1:2] + facts[2:3]
        first, last = facts[3:4], facts[4:5]
        state = state * jnp.where(before == first, 1.0, 0.0)
        entering[s] = bf16(state)
        state = state * jnp.where(first == last, jnp.exp(log_total), 0.0) + f32(arrived[s, 0:32])
        before = last
    for r in FAR_FIRST:
        to = across_plane(seq, *r)
        mail.send(("c", r), entering.at[to], incoming.at[seq], {"seq": to})
    incoming[seq] = entering[seq]
    for r in reversed(FAR_FIRST):
        mail.arrived(("c", r), incoming.at[across_plane(seq, 4 - r[0], 4 - r[1])], {"seq": across_plane(seq, *r)})


def attention_rows(head_out, carry, incoming, attn):
    for h in range(HEADS):
        state = incoming[4 * h : 4 * h + 4].reshape(HS, HS)
        out = head_out[h] + dot(carry[h], state)
        mean = jnp.mean(out * out, axis=1, keepdims=True)
        attn[:, h * HS : (h + 1) * HS] = bf16(out * lax.rsqrt(mean + 1e-05))


HALF = T // 2


class Project:
    def __init__(self, mail, x, c, turn, attn, wo, to_twin, from_twin, part, r1, r2, residual, hidden):
        self.mail, self.c, self.turn, self.attn, self.wo = mail, c, turn, attn, wo
        self.to_twin, self.from_twin, self.part = to_twin.at[turn], from_twin.at[turn], part.at[turn]
        self.r1, self.r2, self.residual, self.hidden = r1.at[turn], r2.at[turn], residual, hidden
        self.twin = {"hx": 2 * x + 1 - c}
        self.up, self.down = {"hx": 2 * ((x + 1) % 4) + c}, {"hx": 2 * ((x + 3) % 4) + c}
        self.lanes = slice(turn * HW, (turn + 1) * HW)

    def product(self, n):
        return dot(self.attn[...], self.wo[n, :, self.lanes]).reshape(2, HALF, HW)

    def send(self, key, src, dst, device):
        self.mail.send((self.turn,) + key, src, dst, device)

    def got(self, key, dst):
        self.mail.arrived((self.turn,) + key, dst, self.up)
        return f32(dst[...])

    def start(self):
        for dx in (2, 1, 3, 0):
            self.to_twin[dx] = bf16(self.product(2 * dx + 1 - self.c))
            self.send(("t", dx), self.to_twin.at[dx], self.from_twin.at[dx], self.twin)

    def both(self, dx):
        return self.product(2 * dx + self.c) + self.got(("t", dx), self.from_twin.at[dx])

    def away(self):
        part = self.part
        part[2] = bf16(self.both(2))
        self.send(("p1", 0), part.at[2, 0], self.r1.at[0], self.up)
        self.send(("p1", 1), part.at[2, 1], self.r1.at[1], self.down)
        mine = self.both(1)
        part[1, 1] = bf16(mine[1])
        self.send(("p2", 0, 1), part.at[1, 1], self.r2.at[0, 1], self.up)
        self.mine_up = mine[0]
        mine = self.both(3)
        part[3, 0] = bf16(mine[0])
        self.send(("p2", 1, 0), part.at[3, 0], self.r2.at[1, 0], self.down)
        self.mine_down = mine[1]
        self.mine = self.both(0)

    def onward(self):
        self.part[1, 0] = bf16(self.mine_up + self.got(("p1", 0), self.r1.at[0]))
        self.send(("p2", 0, 0), self.part.at[1, 0], self.r2.at[0, 0], self.up)
        self.part[3, 1] = bf16(self.mine_down + self.got(("p1", 1), self.r1.at[1]))
        self.send(("p2", 1, 1), self.part.at[3, 1], self.r2.at[1, 1], self.down)

    def home(self):
        for u in (1, 0):
            rows = slice(u * HALF, (u + 1) * HALF)
            total = f32(self.residual[rows, self.lanes]) + self.mine[u]
            total += self.got(("p2", 0, u), self.r2.at[0, u])
            total += self.got(("p2", 1, u), self.r2.at[1, u])
            self.hidden[rows, self.lanes] = total


class Cross:
    def __init__(self, send_sem, recv_sem, number, x, c):
        self.send_sem, self.recv_sem, self.base, self.x, self.c, self.sent = send_sem, recv_sem, 8 * number, x, c, []

    def make(self, dx, to, own, src, dst):
        return pltpu.make_async_remote_copy(
            src_ref=src, dst_ref=dst, send_sem=self.send_sem.at[self.base + 2 * dx + to],
            recv_sem=self.recv_sem.at[self.base + 2 * dx + own], device_id={"hx": 2 * ((self.x + dx) % 4) + to}, device_id_type=MESH)

    def send(self, dx, to, src, dst):
        copy = self.make(dx, to, self.c, src, dst)
        copy.start()
        self.sent.append(copy)

    def arrived(self, dx, own, dst):
        self.make(dx, own, own, dst, dst).wait_recv()

    def drain(self):
        for copy in self.sent:
            copy.wait_send()


def rows_to_experts(cross, facts, x, c, turn, hidden, gain, pick, out, facts_out, block, facts_in):
    hx = 2 * x + c
    own = pl.ds(pl.multiple_of(hx * W + turn * HW, 128), HW)
    rows = bf16(hidden[:, turn * HW : (turn + 1) * HW] * gain[:, own])
    if turn == 1:
        square = jnp.sum(hidden[...] * hidden[...], axis=1, keepdims=True)
        high = f32(bf16(square))
        rows = jnp.concatenate([rows, bf16(jnp.where(iota((T, 128), 1) < 64, high, square - high))], axis=1)
    for dx, to in ((2, 0), (2, 1), (1, 0), (1, 1), (3, 0), (3, 1), (0, 1 - c)):
        n = 2 * dx + (to if dx else 0)
        slots = bf16(dot(pick[2 * ((x + dx) % 4) + to], rows))
        if turn == 1:
            facts_out[n] = slots[:, HW:]
            facts.send(dx, to, facts_out.at[n], facts_in.at[2 * ((4 - dx) % 4) + c])
        out[turn, n] = slots[:, :HW]
        cross.send(dx, to, out.at[turn, n], block.at[position((4 - dx) % 4, turn), c])
    slots = bf16(dot(pick[hx], rows))
    block[position(0, turn), c] = slots[:, :HW]
    if turn == 1:
        facts_in[c] = slots[:, HW:]


def from_row(cross, c, place):
    cross.arrived(0, 1 - c, place(0, 1 - c))
    for dx in (1, 3, 2):
        for own in (0, 1):
            cross.arrived(dx, own, place(4 - dx, own))


def send_scale(mail, seq, facts_in, scale_out, scales):
    square = sum(f32(facts_in[k]) for k in range(SL))
    mean = (square[:, 0:1] + square[:, 64:65]) * (1.0 / (SL * W))
    scale = lax.rsqrt(mean + 1e-06)
    row = jnp.sum(jnp.where(iota((CAP, 128), 0) == iota((CAP, 128), 1), scale, 0.0), axis=0, keepdims=True)
    scale_out[...] = jnp.broadcast_to(row, (8, 128))
    scales[0] = jnp.broadcast_to(row, (8, 128))
    for dy, dz in ORDER[1:]:
        device = {"seq": ((seq // 4 + dy) % 4) * 4 + (seq % 4 + dz) % 4}
        place = SLOT[((4 - dy) % 4, (4 - dz) % 4)]
        mail.send(("n", place), scale_out, scales.at[place], device)


def scale_column(scales, group):
    own = iota((CAP, 128), 0) == iota((CAP, 128), 1)
    return jnp.concatenate(
        [jnp.sum(jnp.where(own, scales[4 * group + b, 0:1, :], 0.0), axis=1, keepdims=True) for b in range(4)], axis=0)


def run_experts(mail, seq, rows, p, wgu, wd, acc, act, scales, r1, r2, q1, q2, loads, out, first_rows, second_rows, finish, combine):
    gathers = [[Gather(mail, rows, half, turn, seq) for half in (0, 1)] for turn in (0, 1)]
    reduces = [[Reduce(mail, p, r1, r2, q1, q2, half, turn, seq) for half in (0, 1)] for turn in (0, 1)]

    def up(group, turn):
        blocks = slice(4 * group, 4 * group + 4)
        parts = [rows[blocks, position(n // 2, turn), n % 2].reshape(4 * CAP, HW) for n in range(SL)]
        block = jnp.concatenate(parts, axis=1)
        total = dot(block, wgu[turn], 1, 1)
        if turn == 0:
            acc[group] = total
        else:
            total = (total + acc[group]) * scale_column(scales, group)
            gate = total[:, 0:F]
            act[group] = bf16(gate / (1.0 + jnp.exp(-gate)) * total[:, F : 2 * F])

    def down(group, turn):
        blocks = slice(4 * group, 4 * group + 4)
        for dx in range(4):
            block = dot(act[group], wd[turn, :, dx * W : (dx + 1) * W])
            for core in (0, 1):
                half = block[:, core * HW : (core + 1) * HW]
                p[blocks, position(dx, turn), core] = bf16(half.reshape(4, CAP, HW))

    def each(step, turn, *args, of=gathers):
        for one in of[turn]:
            getattr(one, step)(*args)

    def reduce(turn, *steps):
        for step in steps:
            each({"s": "start", "m": "middle", "e": "end"}[step[0]], turn, int(step[1]), of=reduces)

    def end(turn):
        for u in (1, 0):
            for half in (1, 0):
                reduces[turn][half].last(u, out)
                finish(2 * half + u, turn)

    first_rows()
    each("start", 0)
    second_rows()
    each("first", 0, 3)
    each("first", 0, 1)
    each("second", 0, 0)
    each("first_far", 0)
    second_rows(True)
    each("start", 1)
    each("second", 0, 3)
    each("second", 0, 1)
    for copy in loads:
        copy.wait()
    up(0, 0)
    each("first", 1, 3)
    each("first", 1, 1)
    each("second", 0, 2)
    each("second", 1, 0)
    up(1, 0)
    for f in (0, 3, 1):
        each("second_far", 0, f)
    each("first_far", 1)
    up(2, 0)
    each("second", 1, 3)
    each("second", 1, 1)
    each("second_far", 0, 2)
    up(3, 0)
    for place in range(1, N_SEQ):
        mail.arrived(("n", place), scales.at[place], {"seq": (seq + 1) % N_SEQ})
    up(0, 1)
    down(0, 0)
    each("second", 1, 2)
    up(1, 1)
    down(1, 0)
    each("second_far", 1, 0)
    each("second_far", 1, 3)
    up(2, 1)
    down(2, 0)
    each("second_far", 1, 1)
    each("second_far", 1, 2)
    up(3, 1)
    down(3, 0)

    reduce(0, "s2", "s1")
    down(0, 1)
    reduce(0, "m2", "s3")
    down(1, 1)
    reduce(0, "m1", "e2", "s0")
    down(2, 1)
    down(3, 1)
    reduce(0, "m3")
    reduce(1, "s2")
    reduce(0, "e1", "m0")
    reduce(1, "s1")
    reduce(0, "e3")
    reduce(1, "m2")
    reduce(0, "e0")
    reduce(1, "s3", "m1")
    end(0)
    reduce(1, "e2", "s0", "m3", "e1", "m0", "e3", "e0")
    combine(0)
    end(1)
    combine(1)


def layer_kernel(q, k, v, decay, docs, residual_in, wo_in, gain, ids, weights, wg_in, wu_in, wd_in, result,
                 wo, residual, pick, shares, states, arrived, entering, incoming, head_out, carry, attn,
                 to_twin, from_twin, part, s1, s2, hidden, slot_out, facts_out, facts_in, scale_out, scales,
                 rows, p, wgu, wd, acc, act, r1, r2, q1, q2, done, back,
                 load_sem, send_sem, recv_sem, cross_send, cross_recv):
    seq, hx = lax.axis_index("seq"), lax.axis_index("hx")
    x, c = hx // 2, hx % 2

    arrive = greet(seq, x, c)
    front, loads = [], []

    def load(copies, source, target):
        n = len(front) + len(loads)
        copies.append(pltpu.make_async_copy(source, target, load_sem.at[n]))
        copies[-1].start()

    for n in range(SL):
        load(front, wo_in.at[:, lanes(2 * ((x + n // 2) % 4) + n % 2)], wo.at[n])
    load(front, residual_in.at[:, lanes(hx)], residual)
    for turn in (0, 1):
        for n in range(SL):
            slice_at = (2 * ((x + n // 2) % 4) + n % 2) * W + turn * HW
            here, target = pl.ds(pl.multiple_of(slice_at, 128), HW), slice(n * HW, (n + 1) * HW)
            load(loads, wg_in.at[:, here], wgu.at[turn, 0:F, target])
            load(loads, wu_in.at[:, here], wgu.at[turn, F : 2 * F, target])
            load(loads, wd_in.at[:, here], wd.at[turn, :, target])

    mail = Mail(send_sem, recv_sem)
    local_attention(q, k, v, decay, docs, states, head_out, carry)
    fill_pick(ids, weights, pick, shares)
    arrive()
    carry_states(mail, seq, states, arrived, entering, incoming)
    attention_rows(head_out, carry, incoming, attn)
    for copy in front:
        copy.wait()
    projects = [Project(mail, x, c, turn, attn, wo, to_twin, from_twin, part, s1, s2, residual, hidden) for turn in (0, 1)]
    crosses = [Cross(cross_send, cross_recv, number, x, c) for number in range(5)]
    own = rows.at[0]

    def dispatch(turn):
        rows_to_experts(crosses[turn], crosses[2], x, c, turn, hidden, gain, pick, slot_out, facts_out, own, facts_in)

    def first_rows():
        projects[0].start()
        projects[0].away()
        projects[1].start()
        projects[0].onward()
        projects[1].away()
        projects[0].home()
        dispatch(0)
        projects[1].onward()
        from_row(crosses[0], c, lambda dx, core: own.at[position(dx, 0), core])

    def second_rows(here=False):
        if here:
            from_row(crosses[2], c, lambda dx, core: facts_in.at[2 * dx + core])
            send_scale(mail, seq, facts_in, scale_out, scales)
            from_row(crosses[1], c, lambda dx, core: own.at[position(dx, 1), core])
        else:
            projects[1].home()
            dispatch(1)

    def finish(dx, turn):
        for to in (0, 1) if dx else (1 - c,):
            crosses[3 + turn].send(dx, to, done.at[position(dx, turn), to], back.at[turn, hx])
        if dx == 0:
            back[turn, hx] = done[position(0, turn), c]

    def combine(turn):
        both = shares[...].reshape(2, SL * CAP, T)
        from_row(crosses[3 + turn], c, lambda dx, core: back.at[turn, 2 * ((x + dx) % 4) + core])
        expert_out = bf16(f32(back[turn]).reshape(SL * CAP, HW))
        half = slice(turn * HW, (turn + 1) * HW)
        result[:, half] = bf16(hidden[:, half] + sum(dot(both[part], expert_out, 0, 0) for part in (0, 1)))

    run_experts(mail, seq, rows, p, wgu, wd, acc, act, scales, r1, r2, q1, q2, loads, done,
                first_rows, second_rows, finish, combine)
    mail.drain()
    for cross in crosses:
        cross.drain()


def fill_pick(ids, weights, pick, shares):
    for e, block in enumerate(dispatch(ids)):
        pick[e] = bf16(block)
        share = jnp.where(ids[0:1, :] == e, weights[0:1, :], 0.0) + jnp.where(ids[1:2, :] == e, weights[1:2, :], 0.0)
        high = bf16(block * share)
        shares[0, e] = high
        shares[1, e] = bf16(block * share - f32(high))


N_MAIL = 30 + 15 + 2 * (4 + 6 + 40 + 48 + 12)


def shards(queries, keys, values, log_decay, doc_ids, residual, out_weight, norm_gain, expert_ids, route_weight, w_gate, w_up, w_down):
    vmem = pl.BlockSpec(memory_space=pltpu.VMEM)
    hbm = pl.BlockSpec(memory_space=pl.ANY)
    bf, fl = jnp.bfloat16, jnp.float32
    dma = pltpu.SemaphoreType.DMA
    unit = (2, CAP, HW)
    scratch = [
        ((SL, HEADS * HS, W), bf), ((T, W), bf), ((SL, CAP, T), bf), ((2, SL, CAP, T), bf),
        ((N_SEQ, 48, HS), bf), ((N_SEQ, 48, HS), bf), ((N_SEQ, 32, HS), bf), ((N_SEQ, 32, HS), bf),
        ((HEADS, T, HS), fl), ((HEADS, T, HS), bf), ((T, HEADS * HS), bf),
        ((2, 4, 2, HALF, HW), bf), ((2, 4, 2, HALF, HW), bf), ((2, 4, 2, HALF, HW), bf),
        ((2, 2, HALF, HW), bf), ((2, 2, 2, HALF, HW), bf),
        ((T, W), fl), ((2, SL, CAP, HW), bf), ((SL, CAP, 128), bf), ((SL, CAP, 128), bf), ((8, 128), fl), ((16, 8, 128), fl),
        ((16, SL) + unit, bf), ((16, SL) + unit, bf), ((2, 2 * F, 4 * W), bf), ((2, F, 4 * W), bf),
        ((4, 4 * CAP, 2 * F), fl), ((4, 4 * CAP, F), bf),
        ((2, 2, 4, 2) + unit, bf), ((2, 2, 4, 2, 2) + unit, bf), ((2, 2, 2) + unit, bf), ((2, 2, 2, 2) + unit, bf),
        ((SL,) + unit, bf), ((2, SL, CAP, HW), bf),
    ]
    return pl.pallas_call(
        layer_kernel,
        out_shape=jax.ShapeDtypeStruct((T, W), bf),
        in_specs=[vmem] * 5 + [hbm, hbm] + [vmem] * 3 + [hbm] * 3,
        out_specs=vmem,
        scratch_shapes=[pltpu.VMEM(*s) for s in scratch]
        + [dma((SL + 1 + 6 * SL,)), dma((N_MAIL,)), dma((N_MAIL,)), dma((40,)), dma((40,))],
        compiler_params=pltpu.CompilerParams(collective_id=0, has_side_effects=True, vmem_limit_bytes=60 * 2**20),
        name="layer",
    )(queries, keys, values, log_decay.T, doc_ids.reshape(1, T), residual, out_weight, norm_gain.reshape(1, SL * W),
      expert_ids.T, route_weight.T, w_gate[0].T, w_up[0].T, w_down[0])


def solution(mesh):
    return jax.shard_map(
        shards,
        mesh=mesh,
        in_specs=(
            P("seq", "hx"),
            P("seq", "hx"),
            P("seq", "hx"),
            P("seq", "hx"),
            P("seq"),
            P("seq", None),
            P("hx", None),
            P(),
            P("seq", None),
            P("seq", None),
            P("hx", None, "seq"),
            P("hx", None, "seq"),
            P("hx", "seq", None),
        ),
        out_specs=P("seq", "hx"),
        check_vma=False,
    )
```

```python
import jax
import jax.numpy as jnp
from jax import lax
from jax.experimental import pallas as pl
from jax.experimental.pallas import tpu as pltpu
from jax.sharding import PartitionSpec as P

MESH = pl.DeviceIdType.MESH
CAP = 40
HS = 128
HEADS = 4
T = 128
N_SEQ = 16
SL = 8
W = 768
HW = W // 2
F = 288
ORDER = [(0, 0), (1, 0), (3, 0), (0, 1), (0, 3), (1, 1), (1, 3), (3, 1), (3, 3), (2, 0), (0, 2), (3, 2), (1, 2), (2, 3), (2, 1), (2, 2)]
SLOT = {r: i for i, r in enumerate(ORDER)}


def at(half, first, second):
    return SLOT[(first % 4, second % 4) if half == 0 else (second % 4, first % 4)]


def across_plane(seq, dy, dz):
    return (seq // 4 + dy) % 4 * 4 + (seq % 4 + dz) % 4


FAR_FIRST = sorted(ORDER[1:], key=lambda r: -(min(r[0], 4 - r[0]) + min(r[1], 4 - r[1])))


class Mail:
    def __init__(self, send_sem, recv_sem):
        self.send_sem, self.recv_sem = send_sem, recv_sem
        self.number, self.sent = {}, []

    def make(self, key, src, dst, device):
        n = self.number.setdefault(key, len(self.number))
        return pltpu.make_async_remote_copy(
            src_ref=src, dst_ref=dst, send_sem=self.send_sem.at[n], recv_sem=self.recv_sem.at[n],
            device_id=device, device_id_type=MESH)

    def send(self, key, src, dst, device):
        copy = self.make(key, src, dst, device)
        copy.start()
        self.sent.append(copy)

    def arrived(self, key, dst, device):
        self.make(key, dst, dst, device).wait_recv()

    def drain(self):
        for copy in self.sent:
            copy.wait_send()


def ring(half, seq):
    y, z = seq // 4, seq % 4
    yp, ym = ((y + 1) % 4) * 4 + z, ((y + 3) % 4) * 4 + z
    zp, zm = y * 4 + (z + 1) % 4, y * 4 + (z + 3) % 4
    ids = (yp, ym, zp, zm) if half == 0 else (zp, zm, yp, ym)
    return [{"seq": i} for i in ids]


def position(dx, turn):
    return 4 * (dx // 2) + dx % 2 + 2 * turn


class Gather:
    def __init__(self, mail, x, half, turn, seq):
        self.mail, self.x, self.half, self.turn = mail, x, half, turn
        self.fp, self.fm, self.sp, self.sm = ring(half, seq)

    def part(self, f, s, unit):
        lo = 4 * self.half + 2 * self.turn
        return self.x.at[at(self.half, f, s), pl.ds(lo, 2) if unit is None else pl.ds(lo + unit, 1)]

    def push(self, f, s, unit, device, tf, ts):
        key = ("g", self.half, self.turn, tf % 4, ts % 4, unit)
        self.mail.send(key, self.part(f, s, unit), self.part(tf, ts, unit), device)

    def got(self, f, s, unit):
        self.mail.arrived(("g", self.half, self.turn, f % 4, s % 4, unit), self.part(f, s, unit), self.fp)

    def across(self, f):
        self.push(f, 0, None, self.sp, f, 3)
        self.push(f, 0, None, self.sm, f, 1)

    def start(self):
        self.push(0, 0, None, self.fp, 3, 0)
        self.push(0, 0, None, self.fm, 1, 0)
        self.across(0)

    def first(self, f):
        self.got(f, 0, None)
        if f == 3:
            self.push(3, 0, 0, self.fp, 2, 0)
        else:
            self.push(1, 0, 1, self.fm, 2, 0)
        self.across(f)

    def first_far(self):
        self.got(2, 0, 0)
        self.got(2, 0, 1)
        self.across(2)

    def second(self, f):
        self.got(f, 3, None)
        self.push(f, 3, 0, self.sp, f, 2)
        self.got(f, 1, None)
        self.push(f, 1, 1, self.sm, f, 2)

    def second_far(self, f):
        self.got(f, 2, 0)
        self.got(f, 2, 1)


class Reduce:
    def __init__(self, mail, p, r1, r2, q1, q2, half, turn, seq):
        self.mail, self.p, self.half, self.turn = mail, p, half, turn
        self.r1, self.r2, self.q1, self.q2 = r1.at[half, turn], r2.at[half, turn], q1.at[half, turn], q2.at[half, turn]
        self.fp, self.fm, self.sp, self.sm = ring(half, seq)

    def unit(self, f, s, u):
        return self.p.at[at(self.half, f, s), 4 * self.half + 2 * self.turn + u]

    def push(self, key, src, dst, device):
        self.mail.send((self.half, self.turn) + key, src, dst, device)

    def got(self, key, dst):
        self.mail.arrived((self.half, self.turn) + key, dst, self.fp)
        return dst

    def total(self, f, s, u, *others):
        total = f32(self.unit(f, s, u)[...])
        for other in others:
            total += f32(other[...])
        return bf16(total)

    def add(self, f, s, u, *others):
        self.unit(f, s, u)[...] = self.total(f, s, u, *others)

    def start(self, f):
        self.push(("r1", f, 0), self.unit(f, 2, 0), self.r1.at[f, 0], self.sp)
        self.push(("r1", f, 1), self.unit(f, 2, 1), self.r1.at[f, 1], self.sm)
        self.push(("r2", f, 0, 1), self.unit(f, 1, 1), self.r2.at[f, 0, 1], self.sp)
        self.push(("r2", f, 1, 0), self.unit(f, 3, 0), self.r2.at[f, 1, 0], self.sm)

    def middle(self, f):
        self.add(f, 1, 0, self.got(("r1", f, 0), self.r1.at[f, 0]))
        self.push(("r2", f, 0, 0), self.unit(f, 1, 0), self.r2.at[f, 0, 0], self.sp)
        self.add(f, 3, 1, self.got(("r1", f, 1), self.r1.at[f, 1]))
        self.push(("r2", f, 1, 1), self.unit(f, 3, 1), self.r2.at[f, 1, 1], self.sm)

    def end(self, f):
        for u in (1, 0) if f == 1 else (0, 1):
            self.add(f, 0, u, self.got(("r2", f, 0, u), self.r2.at[f, 0, u]),
                     self.got(("r2", f, 1, u), self.r2.at[f, 1, u]))
            if f == 2:
                self.push(("q1", u), self.unit(2, 0, u), self.q1.at[u], (self.fp, self.fm)[u])
            if f == 1:
                if u == 0:
                    self.add(1, 0, 0, self.got(("q1", 0), self.q1.at[0]))
                self.push(("q2", 0, u), self.unit(1, 0, u), self.q2.at[0, u], self.fp)
            if f == 3:
                if u == 1:
                    self.add(3, 0, 1, self.got(("q1", 1), self.q1.at[1]))
                self.push(("q2", 1, u), self.unit(3, 0, u), self.q2.at[1, u], self.fm)

    def last(self, u, out):
        a = self.got(("q2", 0, u), self.q2.at[0, u])
        b = self.got(("q2", 1, u), self.q2.at[1, u])
        out[4 * self.half + 2 * self.turn + u] = self.total(0, 0, u, a, b)


def iota(shape, dim):
    return lax.broadcasted_iota(jnp.int32, shape, dim)


def lanes(n):
    return pl.ds(pl.multiple_of(n * W, W), W)


def f32(a):
    return a.astype(jnp.float32)


def bf16(a):
    return a.astype(jnp.bfloat16)


def dot(a, b, ca=1, cb=0, **kw):
    return lax.dot_general(a, b, (((ca,), (cb,)), ((), ())), preferred_element_type=jnp.float32, **kw)


def dispatch(ids):
    experts = iota((SL, T), 0)
    named = (ids[0:1, :] == experts) | (ids[1:2, :] == experts)
    before = bf16(jnp.where(iota((T, T), 0) < iota((T, T), 1), 1.0, 0.0))
    rank = dot(bf16(jnp.where(named, 1.0, 0.0)), before)
    slot = f32(iota((CAP, T), 0))
    chosen = f32(jnp.where(named, 1.0, 0.0))
    return [jnp.where(rank[e : e + 1, :] == slot, 1.0, 0.0) * chosen[e : e + 1, :] for e in range(SL)]


def greet(seq, x, c):
    others = [{"seq": across_plane(seq, *r)} for r in FAR_FIRST]
    others += [{"hx": (2 * x + c + d) % SL} for d in range(1, SL)]
    barrier = pltpu.get_barrier_semaphore()
    for device in others:
        pl.semaphore_signal(barrier, inc=1, device_id=device, device_id_type=MESH)
    return lambda: pl.semaphore_wait(barrier, len(others))


def local_attention(q, k, v, decay, docs, states, head_out, carry):
    doc_row = jnp.broadcast_to(f32(docs[...]), (T, T))
    doc_col = doc_row.T
    allowed = (iota((T, T), 0) >= iota((T, T), 1)) & (doc_row == doc_col)
    upto = f32(jnp.where(iota((T, T), 0) <= iota((T, T), 1), 1.0, 0.0))
    rows = jnp.concatenate([decay[...], jnp.zeros((8 - HEADS, T), jnp.float32)], axis=0)
    sums = dot(rows, upto, precision=lax.Precision.HIGHEST)
    first, last = doc_col[0:1, :], doc_col[T - 1 : T, :]
    row = iota((16, HS), 0)
    for h in range(HEADS):
        lanes = slice(h * HS, (h + 1) * HS)
        across = jnp.broadcast_to(sums[h : h + 1, :], (T, T))
        down = across.T
        fade = jnp.where(allowed, jnp.exp(jnp.where(allowed, down - across, 0.0)), 0.0)
        scores = dot(q[:, lanes], k[:, lanes], 1, 1)
        head_out[h] = dot(bf16(scores * fade), v[:, lanes])
        total = down[T - 1 : T, :]
        to_end = jnp.where(doc_col == last, jnp.exp(total - down), 0.0)
        state = bf16(dot(bf16(f32(k[:, lanes]) * to_end), v[:, lanes], 0, 0))
        carry[h] = bf16(f32(q[:, lanes]) * jnp.where(doc_col == first, jnp.exp(down), 0.0))
        high = f32(bf16(total))
        mid = f32(bf16(total - high))
        low = total - high - mid
        facts = jnp.where(row == 0, high, jnp.where(row == 1, mid, jnp.where(row == 2, low, jnp.where(row == 3, first, last))))
        for part in range(4):
            states[4 * h + part, 0:32] = state[32 * part : 32 * (part + 1)]
            states[4 * h + part, 32:48] = bf16(facts)


def carry_states(mail, seq, states, arrived, entering, incoming):
    for r in FAR_FIRST:
        to = across_plane(seq, *r)
        mail.send(("s", r), states.at[to], arrived.at[seq], {"seq": to})
    arrived[seq] = states[seq]
    for r in reversed(FAR_FIRST):
        mail.arrived(("s", r), arrived.at[across_plane(seq, 4 - r[0], 4 - r[1])], {"seq": across_plane(seq, *r)})
    state = jnp.zeros((32, HS), jnp.float32)
    before = jnp.full((1, HS), -1.0, jnp.float32)
    for s in range(N_SEQ):
        facts = f32(arrived[s, 32:48])
        log_total = facts[0:1] + facts[1:2] + facts[2:3]
        first, last = facts[3:4], facts[4:5]
        state = state * jnp.where(before == first, 1.0, 0.0)
        entering[s] = bf16(state)
        state = state * jnp.where(first == last, jnp.exp(log_total), 0.0) + f32(arrived[s, 0:32])
        before = last
    for r in FAR_FIRST:
        to = across_plane(seq, *r)
        mail.send(("c", r), entering.at[to], incoming.at[seq], {"seq": to})
    incoming[seq] = entering[seq]
    for r in reversed(FAR_FIRST):
        mail.arrived(("c", r), incoming.at[across_plane(seq, 4 - r[0], 4 - r[1])], {"seq": across_plane(seq, *r)})


def attention_rows(head_out, carry, incoming, attn):
    for h in range(HEADS):
        state = incoming[4 * h : 4 * h + 4].reshape(HS, HS)
        out = head_out[h] + dot(carry[h], state)
        mean = jnp.mean(out * out, axis=1, keepdims=True)
        attn[:, h * HS : (h + 1) * HS] = bf16(out * lax.rsqrt(mean + 1e-05))


HALF = T // 2


class Project:
    def __init__(self, mail, x, c, turn, attn, wo, to_twin, from_twin, part, r1, r2, residual, hidden):
        self.mail, self.c, self.turn, self.attn, self.wo = mail, c, turn, attn, wo
        self.to_twin, self.from_twin, self.part = to_twin.at[turn], from_twin.at[turn], part.at[turn]
        self.r1, self.r2, self.residual, self.hidden = r1.at[turn], r2.at[turn], residual, hidden
        self.twin = {"hx": 2 * x + 1 - c}
        self.up, self.down = {"hx": 2 * ((x + 1) % 4) + c}, {"hx": 2 * ((x + 3) % 4) + c}
        self.lanes = slice(turn * HW, (turn + 1) * HW)

    def product(self, n):
        return dot(self.attn[...], self.wo[n, :, self.lanes]).reshape(2, HALF, HW)

    def send(self, key, src, dst, device):
        self.mail.send((self.turn,) + key, src, dst, device)

    def got(self, key, dst):
        self.mail.arrived((self.turn,) + key, dst, self.up)
        return f32(dst[...])

    def start(self):
        for dx in (2, 1, 3, 0):
            self.to_twin[dx] = bf16(self.product(2 * dx + 1 - self.c))
            self.send(("t", dx), self.to_twin.at[dx], self.from_twin.at[dx], self.twin)

    def both(self, dx):
        return self.product(2 * dx + self.c) + self.got(("t", dx), self.from_twin.at[dx])

    def away(self):
        part = self.part
        part[2] = bf16(self.both(2))
        self.send(("p1", 0), part.at[2, 0], self.r1.at[0], self.up)
        self.send(("p1", 1), part.at[2, 1], self.r1.at[1], self.down)
        mine = self.both(1)
        part[1, 1] = bf16(mine[1])
        self.send(("p2", 0, 1), part.at[1, 1], self.r2.at[0, 1], self.up)
        self.mine_up = mine[0]
        mine = self.both(3)
        part[3, 0] = bf16(mine[0])
        self.send(("p2", 1, 0), part.at[3, 0], self.r2.at[1, 0], self.down)
        self.mine_down = mine[1]
        self.mine = self.both(0)

    def onward(self):
        self.part[1, 0] = bf16(self.mine_up + self.got(("p1", 0), self.r1.at[0]))
        self.send(("p2", 0, 0), self.part.at[1, 0], self.r2.at[0, 0], self.up)
        self.part[3, 1] = bf16(self.mine_down + self.got(("p1", 1), self.r1.at[1]))
        self.send(("p2", 1, 1), self.part.at[3, 1], self.r2.at[1, 1], self.down)

    def home(self):
        for u in (1, 0):
            rows = slice(u * HALF, (u + 1) * HALF)
            total = f32(self.residual[rows, self.lanes]) + self.mine[u]
            total += self.got(("p2", 0, u), self.r2.at[0, u])
            total += self.got(("p2", 1, u), self.r2.at[1, u])
            self.hidden[rows, self.lanes] = total


class Cross:
    def __init__(self, send_sem, recv_sem, number, x, c):
        self.send_sem, self.recv_sem, self.base, self.x, self.c, self.sent = send_sem, recv_sem, 8 * number, x, c, []

    def make(self, dx, to, own, src, dst):
        return pltpu.make_async_remote_copy(
            src_ref=src, dst_ref=dst, send_sem=self.send_sem.at[self.base + 2 * dx + to],
            recv_sem=self.recv_sem.at[self.base + 2 * dx + own], device_id={"hx": 2 * ((self.x + dx) % 4) + to}, device_id_type=MESH)

    def send(self, dx, to, src, dst):
        copy = self.make(dx, to, self.c, src, dst)
        copy.start()
        self.sent.append(copy)

    def arrived(self, dx, own, dst):
        self.make(dx, own, own, dst, dst).wait_recv()

    def drain(self):
        for copy in self.sent:
            copy.wait_send()


def rows_to_experts(cross, facts, x, c, turn, hidden, gain, pick, out, facts_out, block, facts_in):
    hx = 2 * x + c
    own = pl.ds(pl.multiple_of(hx * W + turn * HW, 128), HW)
    rows = bf16(hidden[:, turn * HW : (turn + 1) * HW] * gain[:, own])
    if turn == 1:
        square = jnp.sum(hidden[...] * hidden[...], axis=1, keepdims=True)
        high = f32(bf16(square))
        rows = jnp.concatenate([rows, bf16(jnp.where(iota((T, 128), 1) < 64, high, square - high))], axis=1)
    for dx, to in ((2, 0), (2, 1), (1, 0), (1, 1), (3, 0), (3, 1), (0, 1 - c)):
        n = 2 * dx + (to if dx else 0)
        slots = bf16(dot(pick[2 * ((x + dx) % 4) + to], rows))
        if turn == 1:
            facts_out[n] = slots[:, HW:]
            facts.send(dx, to, facts_out.at[n], facts_in.at[2 * ((4 - dx) % 4) + c])
        out[turn, n] = slots[:, :HW]
        cross.send(dx, to, out.at[turn, n], block.at[position((4 - dx) % 4, turn), c])
    slots = bf16(dot(pick[hx], rows))
    block[position(0, turn), c] = slots[:, :HW]
    if turn == 1:
        facts_in[c] = slots[:, HW:]


def from_row(cross, c, place):
    cross.arrived(0, 1 - c, place(0, 1 - c))
    for dx in (1, 3, 2):
        for own in (0, 1):
            cross.arrived(dx, own, place(4 - dx, own))


def send_scale(mail, seq, facts_in, scale_out, scales):
    square = sum(f32(facts_in[k]) for k in range(SL))
    mean = (square[:, 0:1] + square[:, 64:65]) * (1.0 / (SL * W))
    scale = lax.rsqrt(mean + 1e-06)
    row = jnp.sum(jnp.where(iota((CAP, 128), 0) == iota((CAP, 128), 1), scale, 0.0), axis=0, keepdims=True)
    scale_out[...] = jnp.broadcast_to(row, (8, 128))
    scales[0] = jnp.broadcast_to(row, (8, 128))
    for dy, dz in ORDER[1:]:
        device = {"seq": ((seq // 4 + dy) % 4) * 4 + (seq % 4 + dz) % 4}
        place = SLOT[((4 - dy) % 4, (4 - dz) % 4)]
        mail.send(("n", place), scale_out, scales.at[place], device)


def scale_column(scales, group):
    own = iota((CAP, 128), 0) == iota((CAP, 128), 1)
    return jnp.concatenate(
        [jnp.sum(jnp.where(own, scales[4 * group + b, 0:1, :], 0.0), axis=1, keepdims=True) for b in range(4)], axis=0)


def run_experts(mail, seq, rows, p, wgu, wd, acc, act, scales, r1, r2, q1, q2, loads, out, first_rows, second_rows, finish, combine):
    gathers = [[Gather(mail, rows, half, turn, seq) for half in (0, 1)] for turn in (0, 1)]
    reduces = [[Reduce(mail, p, r1, r2, q1, q2, half, turn, seq) for half in (0, 1)] for turn in (0, 1)]

    def up(group, turn):
        blocks = slice(4 * group, 4 * group + 4)
        parts = [rows[blocks, position(n // 2, turn), n % 2].reshape(4 * CAP, HW) for n in range(SL)]
        block = jnp.concatenate(parts, axis=1)
        total = dot(block, wgu[turn], 1, 1)
        if turn == 0:
            acc[group] = total
        else:
            total = (total + acc[group]) * scale_column(scales, group)
            gate = total[:, 0:F]
            act[group] = bf16(gate / (1.0 + jnp.exp(-gate)) * total[:, F : 2 * F])

    def down(group, turn, chips=(0, 1, 2, 3)):
        blocks = slice(4 * group, 4 * group + 4)
        for dx in chips:
            block = dot(act[group], wd[turn, :, dx * W : (dx + 1) * W])
            for core in (0, 1):
                half = block[:, core * HW : (core + 1) * HW]
                p[blocks, position(dx, turn), core] = bf16(half.reshape(4, CAP, HW))

    def each(step, turn, *args, of=gathers):
        for one in of[turn]:
            getattr(one, step)(*args)

    def reduce(turn, *steps):
        for step in steps:
            each({"s": "start", "m": "middle", "e": "end"}[step[0]], turn, int(step[1]), of=reduces)

    def end(turn):
        for u in (1, 0):
            for half in (1, 0):
                reduces[turn][half].last(u, out)
                finish(2 * half + u, turn)

    first_rows()
    each("start", 0)
    second_rows()
    each("first", 0, 3)
    each("first", 0, 1)
    each("second", 0, 0)
    each("first_far", 0)
    second_rows(True)
    each("start", 1)
    each("second", 0, 3)
    each("second", 0, 1)
    for copy in loads:
        copy.wait()
    up(0, 0)
    each("first", 1, 3)
    each("first", 1, 1)
    each("second", 0, 2)
    each("second", 1, 0)
    up(1, 0)
    for f in (0, 3, 1):
        each("second_far", 0, f)
    each("first_far", 1)
    up(2, 0)
    each("second", 1, 3)
    each("second", 1, 1)
    each("second_far", 0, 2)
    up(3, 0)
    for place in range(1, N_SEQ):
        mail.arrived(("n", place), scales.at[place], {"seq": (seq + 1) % N_SEQ})
    up(0, 1)
    down(0, 0)
    each("second", 1, 2)
    up(1, 1)
    down(1, 0)
    each("second_far", 1, 0)
    each("second_far", 1, 3)
    up(2, 1)
    down(2, 0)
    each("second_far", 1, 1)
    each("second_far", 1, 2)
    up(3, 1)
    for half in (0, 1):
        down(3, 0, (2 * half, 2 * half + 1))
        reduces[0][half].start(2)
    reduce(0, "s1")
    down(0, 1)
    reduce(0, "m2", "s3")
    down(1, 1)
    reduce(0, "m1", "e2", "s0")
    down(2, 1)
    down(3, 1)
    reduce(0, "m3")
    reduce(1, "s2")
    reduce(0, "e1", "m0")
    reduce(1, "s1")
    reduce(0, "e3")
    reduce(1, "m2")
    reduce(0, "e0")
    reduce(1, "s3", "m1")
    end(0)
    reduce(1, "e2", "s0", "m3", "e1", "m0", "e3", "e0")
    combine(0)
    end(1)
    combine(1)


def layer_kernel(q, k, v, decay, docs, residual_in, wo_in, gain, ids, weights, wg_in, wu_in, wd_in, result,
                 wo, residual, pick, shares, states, arrived, entering, incoming, head_out, carry, attn,
                 to_twin, from_twin, part, s1, s2, hidden, slot_out, facts_out, facts_in, scale_out, scales,
                 rows, p, wgu, wd, acc, act, r1, r2, q1, q2, done, back,
                 load_sem, send_sem, recv_sem, cross_send, cross_recv):
    seq, hx = lax.axis_index("seq"), lax.axis_index("hx")
    x, c = hx // 2, hx % 2

    arrive = greet(seq, x, c)
    front, loads = [], []

    def load(copies, source, target):
        n = len(front) + len(loads)
        copies.append(pltpu.make_async_copy(source, target, load_sem.at[n]))
        copies[-1].start()

    for n in range(SL):
        load(front, wo_in.at[:, lanes(2 * ((x + n // 2) % 4) + n % 2)], wo.at[n])
    load(front, residual_in.at[:, lanes(hx)], residual)
    for turn in (0, 1):
        for n in range(SL):
            slice_at = (2 * ((x + n // 2) % 4) + n % 2) * W + turn * HW
            here, target = pl.ds(pl.multiple_of(slice_at, 128), HW), slice(n * HW, (n + 1) * HW)
            load(loads, wg_in.at[:, here], wgu.at[turn, 0:F, target])
            load(loads, wu_in.at[:, here], wgu.at[turn, F : 2 * F, target])
            load(loads, wd_in.at[:, here], wd.at[turn, :, target])

    mail = Mail(send_sem, recv_sem)
    local_attention(q, k, v, decay, docs, states, head_out, carry)
    fill_pick(ids, weights, pick, shares)
    arrive()
    carry_states(mail, seq, states, arrived, entering, incoming)
    attention_rows(head_out, carry, incoming, attn)
    for copy in front:
        copy.wait()
    projects = [Project(mail, x, c, turn, attn, wo, to_twin, from_twin, part, s1, s2, residual, hidden) for turn in (0, 1)]
    crosses = [Cross(cross_send, cross_recv, number, x, c) for number in range(5)]
    own = rows.at[0]

    def dispatch(turn):
        rows_to_experts(crosses[turn], crosses[2], x, c, turn, hidden, gain, pick, slot_out, facts_out, own, facts_in)

    def first_rows():
        projects[0].start()
        projects[0].away()
        projects[1].start()
        projects[0].onward()
        projects[1].away()
        projects[0].home()
        dispatch(0)
        projects[1].onward()
        from_row(crosses[0], c, lambda dx, core: own.at[position(dx, 0), core])

    def second_rows(here=False):
        if here:
            from_row(crosses[2], c, lambda dx, core: facts_in.at[2 * dx + core])
            send_scale(mail, seq, facts_in, scale_out, scales)
            from_row(crosses[1], c, lambda dx, core: own.at[position(dx, 1), core])
        else:
            projects[1].home()
            dispatch(1)

    def finish(dx, turn):
        for to in (0, 1) if dx else (1 - c,):
            crosses[3 + turn].send(dx, to, done.at[position(dx, turn), to], back.at[turn, hx])
        if dx == 0:
            back[turn, hx] = done[position(0, turn), c]

    def combine(turn):
        both = shares[...].reshape(2, SL * CAP, T)
        from_row(crosses[3 + turn], c, lambda dx, core: back.at[turn, 2 * ((x + dx) % 4) + core])
        expert_out = bf16(f32(back[turn]).reshape(SL * CAP, HW))
        half = slice(turn * HW, (turn + 1) * HW)
        result[:, half] = bf16(hidden[:, half] + sum(dot(both[part], expert_out, 0, 0) for part in (0, 1)))

    run_experts(mail, seq, rows, p, wgu, wd, acc, act, scales, r1, r2, q1, q2, loads, done,
                first_rows, second_rows, finish, combine)
    mail.drain()
    for cross in crosses:
        cross.drain()


def fill_pick(ids, weights, pick, shares):
    for e, block in enumerate(dispatch(ids)):
        pick[e] = bf16(block)
        share = jnp.where(ids[0:1, :] == e, weights[0:1, :], 0.0) + jnp.where(ids[1:2, :] == e, weights[1:2, :], 0.0)
        high = bf16(block * share)
        shares[0, e] = high
        shares[1, e] = bf16(block * share - f32(high))


N_MAIL = 30 + 15 + 2 * (4 + 6 + 40 + 48 + 12)


def shards(queries, keys, values, log_decay, doc_ids, residual, out_weight, norm_gain, expert_ids, route_weight, w_gate, w_up, w_down):
    vmem = pl.BlockSpec(memory_space=pltpu.VMEM)
    hbm = pl.BlockSpec(memory_space=pl.ANY)
    bf, fl = jnp.bfloat16, jnp.float32
    dma = pltpu.SemaphoreType.DMA
    unit = (2, CAP, HW)
    scratch = [
        ((SL, HEADS * HS, W), bf), ((T, W), bf), ((SL, CAP, T), bf), ((2, SL, CAP, T), bf),
        ((N_SEQ, 48, HS), bf), ((N_SEQ, 48, HS), bf), ((N_SEQ, 32, HS), bf), ((N_SEQ, 32, HS), bf),
        ((HEADS, T, HS), fl), ((HEADS, T, HS), bf), ((T, HEADS * HS), bf),
        ((2, 4, 2, HALF, HW), bf), ((2, 4, 2, HALF, HW), bf), ((2, 4, 2, HALF, HW), bf),
        ((2, 2, HALF, HW), bf), ((2, 2, 2, HALF, HW), bf),
        ((T, W), fl), ((2, SL, CAP, HW), bf), ((SL, CAP, 128), bf), ((SL, CAP, 128), bf), ((8, 128), fl), ((16, 8, 128), fl),
        ((16, SL) + unit, bf), ((16, SL) + unit, bf), ((2, 2 * F, 4 * W), bf), ((2, F, 4 * W), bf),
        ((4, 4 * CAP, 2 * F), fl), ((4, 4 * CAP, F), bf),
        ((2, 2, 4, 2) + unit, bf), ((2, 2, 4, 2, 2) + unit, bf), ((2, 2, 2) + unit, bf), ((2, 2, 2, 2) + unit, bf),
        ((SL,) + unit, bf), ((2, SL, CAP, HW), bf),
    ]
    return pl.pallas_call(
        layer_kernel,
        out_shape=jax.ShapeDtypeStruct((T, W), bf),
        in_specs=[vmem] * 5 + [hbm, hbm] + [vmem] * 3 + [hbm] * 3,
        out_specs=vmem,
        scratch_shapes=[pltpu.VMEM(*s) for s in scratch]
        + [dma((SL + 1 + 6 * SL,)), dma((N_MAIL,)), dma((N_MAIL,)), dma((40,)), dma((40,))],
        compiler_params=pltpu.CompilerParams(collective_id=0, has_side_effects=True, vmem_limit_bytes=60 * 2**20),
        name="layer",
    )(queries, keys, values, log_decay.T, doc_ids.reshape(1, T), residual, out_weight, norm_gain.reshape(1, SL * W),
      expert_ids.T, route_weight.T, w_gate[0].T, w_up[0].T, w_down[0])


def solution(mesh):
    return jax.shard_map(
        shards,
        mesh=mesh,
        in_specs=(
            P("seq", "hx"),
            P("seq", "hx"),
            P("seq", "hx"),
            P("seq", "hx"),
            P("seq"),
            P("seq", None),
            P("hx", None),
            P(),
            P("seq", None),
            P("seq", None),
            P("hx", None, "seq"),
            P("hx", None, "seq"),
            P("hx", "seq", None),
        ),
        out_specs=P("seq", "hx"),
        check_vma=False,
    )
```

```python
import jax
import jax.numpy as jnp
from jax import lax
from jax.experimental import pallas as pl
from jax.experimental.pallas import tpu as pltpu
from jax.sharding import PartitionSpec as P

MESH = pl.DeviceIdType.MESH
CAP = 40
HS = 128
HEADS = 4
T = 128
N_SEQ = 16
SL = 8
W = 768
HW = W // 2
F = 288
ORDER = [(0, 0), (1, 0), (3, 0), (0, 1), (0, 3), (1, 1), (1, 3), (3, 1), (3, 3), (2, 0), (0, 2), (3, 2), (1, 2), (2, 3), (2, 1), (2, 2)]
SLOT = {r: i for i, r in enumerate(ORDER)}


def at(half, first, second):
    return SLOT[(first % 4, second % 4) if half == 0 else (second % 4, first % 4)]


def across_plane(seq, dy, dz):
    return (seq // 4 + dy) % 4 * 4 + (seq % 4 + dz) % 4


FAR_FIRST = sorted(ORDER[1:], key=lambda r: -(min(r[0], 4 - r[0]) + min(r[1], 4 - r[1])))


class Mail:
    def __init__(self, send_sem, recv_sem):
        self.send_sem, self.recv_sem = send_sem, recv_sem
        self.number, self.sent = {}, []

    def make(self, key, src, dst, device):
        n = self.number.setdefault(key, len(self.number))
        return pltpu.make_async_remote_copy(
            src_ref=src, dst_ref=dst, send_sem=self.send_sem.at[n], recv_sem=self.recv_sem.at[n],
            device_id=device, device_id_type=MESH)

    def send(self, key, src, dst, device):
        copy = self.make(key, src, dst, device)
        copy.start()
        self.sent.append(copy)

    def arrived(self, key, dst, device):
        self.make(key, dst, dst, device).wait_recv()

    def drain(self):
        for copy in self.sent:
            copy.wait_send()


def ring(half, seq):
    y, z = seq // 4, seq % 4
    yp, ym = ((y + 1) % 4) * 4 + z, ((y + 3) % 4) * 4 + z
    zp, zm = y * 4 + (z + 1) % 4, y * 4 + (z + 3) % 4
    ids = (yp, ym, zp, zm) if half == 0 else (zp, zm, yp, ym)
    return [{"seq": i} for i in ids]


def position(dx, turn):
    return 4 * (dx // 2) + dx % 2 + 2 * turn


class Gather:
    def __init__(self, mail, x, half, turn, seq):
        self.mail, self.x, self.half, self.turn = mail, x, half, turn
        self.fp, self.fm, self.sp, self.sm = ring(half, seq)

    def part(self, f, s, unit):
        lo = 4 * self.half + 2 * self.turn
        return self.x.at[at(self.half, f, s), pl.ds(lo, 2) if unit is None else pl.ds(lo + unit, 1)]

    def push(self, f, s, unit, device, tf, ts):
        key = ("g", self.half, self.turn, tf % 4, ts % 4, unit)
        self.mail.send(key, self.part(f, s, unit), self.part(tf, ts, unit), device)

    def got(self, f, s, unit):
        self.mail.arrived(("g", self.half, self.turn, f % 4, s % 4, unit), self.part(f, s, unit), self.fp)

    def across(self, f):
        self.push(f, 0, None, self.sp, f, 3)
        self.push(f, 0, None, self.sm, f, 1)

    def start(self):
        self.push(0, 0, None, self.fp, 3, 0)
        self.push(0, 0, None, self.fm, 1, 0)
        self.across(0)

    def first(self, f):
        self.got(f, 0, None)
        if f == 3:
            self.push(3, 0, 0, self.fp, 2, 0)
        else:
            self.push(1, 0, 1, self.fm, 2, 0)
        self.across(f)

    def first_far(self):
        self.got(2, 0, 0)
        self.got(2, 0, 1)
        self.across(2)

    def second(self, f):
        self.got(f, 3, None)
        self.push(f, 3, 0, self.sp, f, 2)
        self.got(f, 1, None)
        self.push(f, 1, 1, self.sm, f, 2)

    def second_far(self, f):
        self.got(f, 2, 0)
        self.got(f, 2, 1)


class Reduce:
    def __init__(self, mail, p, r1, r2, q1, q2, half, turn, seq):
        self.mail, self.p, self.half, self.turn = mail, p, half, turn
        self.r1, self.r2, self.q1, self.q2 = r1.at[half, turn], r2.at[half, turn], q1.at[half, turn], q2.at[half, turn]
        self.fp, self.fm, self.sp, self.sm = ring(half, seq)

    def unit(self, f, s, u):
        return self.p.at[at(self.half, f, s), 4 * self.half + 2 * self.turn + u]

    def push(self, key, src, dst, device):
        self.mail.send((self.half, self.turn) + key, src, dst, device)

    def got(self, key, dst):
        self.mail.arrived((self.half, self.turn) + key, dst, self.fp)
        return dst

    def total(self, f, s, u, *others):
        total = f32(self.unit(f, s, u)[...])
        for other in others:
            total += f32(other[...])
        return bf16(total)

    def add(self, f, s, u, *others):
        self.unit(f, s, u)[...] = self.total(f, s, u, *others)

    def start(self, f):
        self.push(("r1", f, 0), self.unit(f, 2, 0), self.r1.at[f, 0], self.sp)
        self.push(("r1", f, 1), self.unit(f, 2, 1), self.r1.at[f, 1], self.sm)
        self.push(("r2", f, 0, 1), self.unit(f, 1, 1), self.r2.at[f, 0, 1], self.sp)
        self.push(("r2", f, 1, 0), self.unit(f, 3, 0), self.r2.at[f, 1, 0], self.sm)

    def middle(self, f):
        self.add(f, 1, 0, self.got(("r1", f, 0), self.r1.at[f, 0]))
        self.push(("r2", f, 0, 0), self.unit(f, 1, 0), self.r2.at[f, 0, 0], self.sp)
        self.add(f, 3, 1, self.got(("r1", f, 1), self.r1.at[f, 1]))
        self.push(("r2", f, 1, 1), self.unit(f, 3, 1), self.r2.at[f, 1, 1], self.sm)

    def end(self, f):
        for u in (1, 0) if f == 1 else (0, 1):
            self.add(f, 0, u, self.got(("r2", f, 0, u), self.r2.at[f, 0, u]),
                     self.got(("r2", f, 1, u), self.r2.at[f, 1, u]))
            if f == 2:
                self.push(("q1", u), self.unit(2, 0, u), self.q1.at[u], (self.fp, self.fm)[u])
            if f == 1:
                if u == 0:
                    self.add(1, 0, 0, self.got(("q1", 0), self.q1.at[0]))
                self.push(("q2", 0, u), self.unit(1, 0, u), self.q2.at[0, u], self.fp)
            if f == 3:
                if u == 1:
                    self.add(3, 0, 1, self.got(("q1", 1), self.q1.at[1]))
                self.push(("q2", 1, u), self.unit(3, 0, u), self.q2.at[1, u], self.fm)

    def last(self, u, out):
        a = self.got(("q2", 0, u), self.q2.at[0, u])
        b = self.got(("q2", 1, u), self.q2.at[1, u])
        out[4 * self.half + 2 * self.turn + u] = self.total(0, 0, u, a, b)


def iota(shape, dim):
    return lax.broadcasted_iota(jnp.int32, shape, dim)


def lanes(n):
    return pl.ds(pl.multiple_of(n * W, W), W)


def f32(a):
    return a.astype(jnp.float32)


def bf16(a):
    return a.astype(jnp.bfloat16)


def dot(a, b, ca=1, cb=0, **kw):
    return lax.dot_general(a, b, (((ca,), (cb,)), ((), ())), preferred_element_type=jnp.float32, **kw)


def dispatch(ids):
    experts = iota((SL, T), 0)
    named = (ids[0:1, :] == experts) | (ids[1:2, :] == experts)
    before = bf16(jnp.where(iota((T, T), 0) < iota((T, T), 1), 1.0, 0.0))
    rank = dot(bf16(jnp.where(named, 1.0, 0.0)), before)
    slot = f32(iota((CAP, T), 0))
    chosen = f32(jnp.where(named, 1.0, 0.0))
    return [jnp.where(rank[e : e + 1, :] == slot, 1.0, 0.0) * chosen[e : e + 1, :] for e in range(SL)]


def greet(seq, x, c):
    others = [{"seq": across_plane(seq, *r)} for r in FAR_FIRST]
    others += [{"hx": (2 * x + c + d) % SL} for d in range(1, SL)]
    barrier = pltpu.get_barrier_semaphore()
    for device in others:
        pl.semaphore_signal(barrier, inc=1, device_id=device, device_id_type=MESH)
    return lambda: pl.semaphore_wait(barrier, len(others))


def local_attention(q, k, v, decay, docs, states, head_out, carry):
    doc_row = jnp.broadcast_to(f32(docs[...]), (T, T))
    doc_col = doc_row.T
    allowed = (iota((T, T), 0) >= iota((T, T), 1)) & (doc_row == doc_col)
    upto = f32(jnp.where(iota((T, T), 0) <= iota((T, T), 1), 1.0, 0.0))
    rows = jnp.concatenate([decay[...], jnp.zeros((8 - HEADS, T), jnp.float32)], axis=0)
    sums = dot(rows, upto, precision=lax.Precision.HIGHEST)
    first, last = doc_col[0:1, :], doc_col[T - 1 : T, :]
    row = iota((16, HS), 0)
    for h in range(HEADS):
        lanes = slice(h * HS, (h + 1) * HS)
        across = jnp.broadcast_to(sums[h : h + 1, :], (T, T))
        down = across.T
        fade = jnp.where(allowed, jnp.exp(jnp.where(allowed, down - across, 0.0)), 0.0)
        scores = dot(q[:, lanes], k[:, lanes], 1, 1)
        head_out[h] = dot(bf16(scores * fade), v[:, lanes])
        total = down[T - 1 : T, :]
        to_end = jnp.where(doc_col == last, jnp.exp(total - down), 0.0)
        state = bf16(dot(bf16(f32(k[:, lanes]) * to_end), v[:, lanes], 0, 0))
        carry[h] = bf16(f32(q[:, lanes]) * jnp.where(doc_col == first, jnp.exp(down), 0.0))
        high = f32(bf16(total))
        mid = f32(bf16(total - high))
        low = total - high - mid
        facts = jnp.where(row == 0, high, jnp.where(row == 1, mid, jnp.where(row == 2, low, jnp.where(row == 3, first, last))))
        for part in range(4):
            states[4 * h + part, 0:32] = state[32 * part : 32 * (part + 1)]
            states[4 * h + part, 32:48] = bf16(facts)


def carry_states(mail, seq, states, arrived, entering, incoming):
    for r in FAR_FIRST:
        to = across_plane(seq, *r)
        mail.send(("s", r), states.at[to], arrived.at[seq], {"seq": to})
    arrived[seq] = states[seq]
    for r in reversed(FAR_FIRST):
        mail.arrived(("s", r), arrived.at[across_plane(seq, 4 - r[0], 4 - r[1])], {"seq": across_plane(seq, *r)})
    state = jnp.zeros((32, HS), jnp.float32)
    before = jnp.full((1, HS), -1.0, jnp.float32)
    for s in range(N_SEQ):
        facts = f32(arrived[s, 32:48])
        log_total = facts[0:1] + facts[1:2] + facts[2:3]
        first, last = facts[3:4], facts[4:5]
        state = state * jnp.where(before == first, 1.0, 0.0)
        entering[s] = bf16(state)
        state = state * jnp.where(first == last, jnp.exp(log_total), 0.0) + f32(arrived[s, 0:32])
        before = last
    for r in FAR_FIRST:
        to = across_plane(seq, *r)
        mail.send(("c", r), entering.at[to], incoming.at[seq], {"seq": to})
    incoming[seq] = entering[seq]
    for r in reversed(FAR_FIRST):
        mail.arrived(("c", r), incoming.at[across_plane(seq, 4 - r[0], 4 - r[1])], {"seq": across_plane(seq, *r)})


def attention_rows(head_out, carry, incoming, attn):
    for h in range(HEADS):
        state = incoming[4 * h : 4 * h + 4].reshape(HS, HS)
        out = head_out[h] + dot(carry[h], state)
        mean = jnp.mean(out * out, axis=1, keepdims=True)
        attn[:, h * HS : (h + 1) * HS] = bf16(out * lax.rsqrt(mean + 1e-05))


HALF = T // 2


class Project:
    def __init__(self, mail, x, c, turn, attn, wo, to_twin, from_twin, part, r1, r2, residual, hidden):
        self.mail, self.c, self.turn, self.attn, self.wo = mail, c, turn, attn, wo
        self.to_twin, self.from_twin, self.part = to_twin.at[turn], from_twin.at[turn], part.at[turn]
        self.r1, self.r2, self.residual, self.hidden = r1.at[turn], r2.at[turn], residual, hidden
        self.twin = {"hx": 2 * x + 1 - c}
        self.up, self.down = {"hx": 2 * ((x + 1) % 4) + c}, {"hx": 2 * ((x + 3) % 4) + c}
        self.lanes = slice(turn * HW, (turn + 1) * HW)

    def product(self, n):
        return dot(self.attn[...], self.wo[n, :, self.lanes]).reshape(2, HALF, HW)

    def send(self, key, src, dst, device):
        self.mail.send((self.turn,) + key, src, dst, device)

    def got(self, key, dst):
        self.mail.arrived((self.turn,) + key, dst, self.up)
        return f32(dst[...])

    def start(self):
        for dx in (2, 1, 3, 0):
            self.to_twin[dx] = bf16(self.product(2 * dx + 1 - self.c))
            self.send(("t", dx), self.to_twin.at[dx], self.from_twin.at[dx], self.twin)

    def both(self, dx):
        return self.product(2 * dx + self.c) + self.got(("t", dx), self.from_twin.at[dx])

    def away(self):
        part = self.part
        part[2] = bf16(self.both(2))
        self.send(("p1", 0), part.at[2, 0], self.r1.at[0], self.up)
        self.send(("p1", 1), part.at[2, 1], self.r1.at[1], self.down)
        mine = self.both(1)
        part[1, 1] = bf16(mine[1])
        self.send(("p2", 0, 1), part.at[1, 1], self.r2.at[0, 1], self.up)
        self.mine_up = mine[0]
        mine = self.both(3)
        part[3, 0] = bf16(mine[0])
        self.send(("p2", 1, 0), part.at[3, 0], self.r2.at[1, 0], self.down)
        self.mine_down = mine[1]
        self.mine = self.both(0)

    def onward(self):
        self.part[1, 0] = bf16(self.mine_up + self.got(("p1", 0), self.r1.at[0]))
        self.send(("p2", 0, 0), self.part.at[1, 0], self.r2.at[0, 0], self.up)
        self.part[3, 1] = bf16(self.mine_down + self.got(("p1", 1), self.r1.at[1]))
        self.send(("p2", 1, 1), self.part.at[3, 1], self.r2.at[1, 1], self.down)

    def home(self):
        for u in (1, 0):
            rows = slice(u * HALF, (u + 1) * HALF)
            total = f32(self.residual[rows, self.lanes]) + self.mine[u]
            total += self.got(("p2", 0, u), self.r2.at[0, u])
            total += self.got(("p2", 1, u), self.r2.at[1, u])
            self.hidden[rows, self.lanes] = total


class Cross:
    def __init__(self, send_sem, recv_sem, number, x, c):
        self.send_sem, self.recv_sem, self.base, self.x, self.c, self.sent = send_sem, recv_sem, 8 * number, x, c, []

    def make(self, dx, to, own, src, dst):
        return pltpu.make_async_remote_copy(
            src_ref=src, dst_ref=dst, send_sem=self.send_sem.at[self.base + 2 * dx + to],
            recv_sem=self.recv_sem.at[self.base + 2 * dx + own], device_id={"hx": 2 * ((self.x + dx) % 4) + to}, device_id_type=MESH)

    def send(self, dx, to, src, dst):
        copy = self.make(dx, to, self.c, src, dst)
        copy.start()
        self.sent.append(copy)

    def arrived(self, dx, own, dst):
        self.make(dx, own, own, dst, dst).wait_recv()

    def drain(self):
        for copy in self.sent:
            copy.wait_send()


def rows_to_experts(cross, facts, x, c, turn, hidden, gain, pick, out, facts_out, block, facts_in):
    hx = 2 * x + c
    own = pl.ds(pl.multiple_of(hx * W + turn * HW, 128), HW)
    rows = bf16(hidden[:, turn * HW : (turn + 1) * HW] * gain[:, own])
    if turn == 1:
        square = jnp.sum(hidden[...] * hidden[...], axis=1, keepdims=True)
        high = f32(bf16(square))
        rows = jnp.concatenate([rows, bf16(jnp.where(iota((T, 128), 1) < 64, high, square - high))], axis=1)
    for dx, to in ((2, 0), (2, 1), (1, 0), (1, 1), (3, 0), (3, 1), (0, 1 - c)):
        n = 2 * dx + (to if dx else 0)
        slots = bf16(dot(pick[2 * ((x + dx) % 4) + to], rows))
        if turn == 1:
            facts_out[n] = slots[:, HW:]
            facts.send(dx, to, facts_out.at[n], facts_in.at[2 * ((4 - dx) % 4) + c])
        out[turn, n] = slots[:, :HW]
        cross.send(dx, to, out.at[turn, n], block.at[position((4 - dx) % 4, turn), c])
    slots = bf16(dot(pick[hx], rows))
    block[position(0, turn), c] = slots[:, :HW]
    if turn == 1:
        facts_in[c] = slots[:, HW:]


def from_row(cross, c, place):
    cross.arrived(0, 1 - c, place(0, 1 - c))
    for dx in (1, 3, 2):
        for own in (0, 1):
            cross.arrived(dx, own, place(4 - dx, own))


def send_scale(mail, seq, facts_in, scale_out, scales):
    square = sum(f32(facts_in[k]) for k in range(SL))
    mean = (square[:, 0:1] + square[:, 64:65]) * (1.0 / (SL * W))
    scale = lax.rsqrt(mean + 1e-06)
    row = jnp.sum(jnp.where(iota((CAP, 128), 0) == iota((CAP, 128), 1), scale, 0.0), axis=0, keepdims=True)
    scale_out[...] = jnp.broadcast_to(row, (8, 128))
    scales[0] = jnp.broadcast_to(row, (8, 128))
    for dy, dz in ORDER[1:]:
        device = {"seq": ((seq // 4 + dy) % 4) * 4 + (seq % 4 + dz) % 4}
        place = SLOT[((4 - dy) % 4, (4 - dz) % 4)]
        mail.send(("n", place), scale_out, scales.at[place], device)


def scale_column(scales, group):
    own = iota((CAP, 128), 0) == iota((CAP, 128), 1)
    return jnp.concatenate(
        [jnp.sum(jnp.where(own, scales[4 * group + b, 0:1, :], 0.0), axis=1, keepdims=True) for b in range(4)], axis=0)


def run_experts(mail, seq, rows, p, wgu, wd, acc, act, scales, r1, r2, q1, q2, loads, out, first_rows, second_rows, finish, combine):
    gathers = [[Gather(mail, rows, half, turn, seq) for half in (0, 1)] for turn in (0, 1)]
    reduces = [[Reduce(mail, p, r1, r2, q1, q2, half, turn, seq) for half in (0, 1)] for turn in (0, 1)]

    def up(group, turn):
        blocks = slice(4 * group, 4 * group + 4)
        parts = [rows[blocks, position(n // 2, turn), n % 2].reshape(4 * CAP, HW) for n in range(SL)]
        block = jnp.concatenate(parts, axis=1)
        total = dot(block, wgu[turn], 1, 1)
        if turn == 0:
            acc[group] = total
        else:
            total = (total + acc[group]) * scale_column(scales, group)
            gate = total[:, 0:F]
            act[group] = bf16(gate / (1.0 + jnp.exp(-gate)) * total[:, F : 2 * F])

    def down(group, turn):
        blocks = slice(4 * group, 4 * group + 4)
        for dx in range(4):
            block = dot(act[group], wd[turn, :, dx * W : (dx + 1) * W])
            for core in (0, 1):
                half = block[:, core * HW : (core + 1) * HW]
                p[blocks, position(dx, turn), core] = bf16(half.reshape(4, CAP, HW))

    def each(step, turn, *args, of=gathers):
        for one in of[turn]:
            getattr(one, step)(*args)

    def reduce(turn, *steps):
        for step in steps:
            each({"s": "start", "m": "middle", "e": "end"}[step[0]], turn, int(step[1]), of=reduces)

    def end(turn):
        for u in (1, 0):
            for half in (1, 0):
                reduces[turn][half].last(u, out)
                finish(2 * half + u, turn)

    first_rows()
    each("start", 0)
    second_rows()
    each("first", 0, 3)
    each("first", 0, 1)
    each("second", 0, 0)
    each("first_far", 0)
    second_rows(True)
    each("start", 1)
    each("second", 0, 3)
    each("second", 0, 1)
    for copy in loads:
        copy.wait()
    up(0, 0)
    each("first", 1, 3)
    each("first", 1, 1)
    each("second", 0, 2)
    each("second", 1, 0)
    up(1, 0)
    for f in (0, 3, 1):
        each("second_far", 0, f)
    each("first_far", 1)
    up(2, 0)
    each("second", 1, 3)
    each("second", 1, 1)
    each("second_far", 0, 2)
    up(3, 0)
    for place in range(1, N_SEQ):
        mail.arrived(("n", place), scales.at[place], {"seq": (seq + 1) % N_SEQ})
    up(0, 1)
    down(0, 0)
    each("second", 1, 2)
    up(1, 1)
    down(1, 0)
    each("second_far", 1, 0)
    each("second_far", 1, 3)
    up(2, 1)
    down(2, 0)
    each("second_far", 1, 1)
    each("second_far", 1, 2)
    up(3, 1)
    down(3, 0)

    reduce(0, "s2", "s1")
    down(0, 1)
    reduce(0, "m2", "s3")
    down(1, 1)
    reduce(0, "m1", "e2", "s0")
    down(2, 1)
    down(3, 1)
    reduce(0, "m3")
    reduce(1, "s2")
    reduce(0, "e1", "m0")
    reduce(1, "s1")
    reduce(0, "e3")
    reduce(1, "m2")
    reduce(0, "e0")
    reduce(1, "s3", "m1")
    end(0)
    reduce(1, "e2", "s0", "m3", "e1", "m0", "e3", "e0")
    combine(0)
    end(1)
    combine(1)


def layer_kernel(q_in, k_in, v_in, decay_in, docs_in, residual_in, wo_in, gain_in, ids_in, weights_in, wg_in, wu_in, wd_in, result,
                 q, k, v, decay, docs, gain, ids, weights, wo, residual, pick, shares, states, arrived, entering, incoming, head_out, carry, attn,
                 to_twin, from_twin, part, s1, s2, hidden, slot_out, facts_out, facts_in, scale_out, scales,
                 rows, p, wgu, wd, acc, act, r1, r2, q1, q2, done, back,
                 load_sem, send_sem, recv_sem, cross_send, cross_recv):
    seq, hx = lax.axis_index("seq"), lax.axis_index("hx")
    x, c = hx // 2, hx % 2

    arrive = greet(seq, x, c)
    early, front, loads = [], [], []

    def load(copies, source, target):
        n = len(early) + len(front) + len(loads)
        copies.append(pltpu.make_async_copy(source, target, load_sem.at[n]))
        copies[-1].start()

    sources = (q_in, k_in, v_in, decay_in, docs_in, gain_in, ids_in, weights_in)
    for source, target in zip(sources, (q, k, v, decay, docs, gain, ids, weights)):
        load(early, source, target)
    for n in range(SL):
        load(front, wo_in.at[:, lanes(2 * ((x + n // 2) % 4) + n % 2)], wo.at[n])
    load(front, residual_in.at[:, lanes(hx)], residual)
    for turn in (0, 1):
        for n in range(SL):
            slice_at = (2 * ((x + n // 2) % 4) + n % 2) * W + turn * HW
            here, target = pl.ds(pl.multiple_of(slice_at, 128), HW), slice(n * HW, (n + 1) * HW)
            load(loads, wg_in.at[:, here], wgu.at[turn, 0:F, target])
            load(loads, wu_in.at[:, here], wgu.at[turn, F : 2 * F, target])
            load(loads, wd_in.at[:, here], wd.at[turn, :, target])

    mail = Mail(send_sem, recv_sem)
    for copy in early:
        copy.wait()
    local_attention(q, k, v, decay, docs, states, head_out, carry)
    fill_pick(ids, weights, pick, shares)
    arrive()
    carry_states(mail, seq, states, arrived, entering, incoming)
    attention_rows(head_out, carry, incoming, attn)
    for copy in front:
        copy.wait()
    projects = [Project(mail, x, c, turn, attn, wo, to_twin, from_twin, part, s1, s2, residual, hidden) for turn in (0, 1)]
    crosses = [Cross(cross_send, cross_recv, number, x, c) for number in range(5)]
    own = rows.at[0]

    def dispatch(turn):
        rows_to_experts(crosses[turn], crosses[2], x, c, turn, hidden, gain, pick, slot_out, facts_out, own, facts_in)

    def first_rows():
        projects[0].start()
        projects[0].away()
        projects[1].start()
        projects[0].onward()
        projects[1].away()
        projects[0].home()
        dispatch(0)
        projects[1].onward()
        from_row(crosses[0], c, lambda dx, core: own.at[position(dx, 0), core])

    def second_rows(here=False):
        if here:
            from_row(crosses[2], c, lambda dx, core: facts_in.at[2 * dx + core])
            send_scale(mail, seq, facts_in, scale_out, scales)
            from_row(crosses[1], c, lambda dx, core: own.at[position(dx, 1), core])
        else:
            projects[1].home()
            dispatch(1)

    def finish(dx, turn):
        for to in (0, 1) if dx else (1 - c,):
            crosses[3 + turn].send(dx, to, done.at[position(dx, turn), to], back.at[turn, hx])
        if dx == 0:
            back[turn, hx] = done[position(0, turn), c]

    def combine(turn):
        both = shares[...].reshape(2, SL * CAP, T)
        from_row(crosses[3 + turn], c, lambda dx, core: back.at[turn, 2 * ((x + dx) % 4) + core])
        expert_out = bf16(f32(back[turn]).reshape(SL * CAP, HW))
        half = slice(turn * HW, (turn + 1) * HW)
        result[:, half] = bf16(hidden[:, half] + sum(dot(both[part], expert_out, 0, 0) for part in (0, 1)))

    run_experts(mail, seq, rows, p, wgu, wd, acc, act, scales, r1, r2, q1, q2, loads, done,
                first_rows, second_rows, finish, combine)
    mail.drain()
    for cross in crosses:
        cross.drain()


def fill_pick(ids, weights, pick, shares):
    for e, block in enumerate(dispatch(ids)):
        pick[e] = bf16(block)
        share = jnp.where(ids[0:1, :] == e, weights[0:1, :], 0.0) + jnp.where(ids[1:2, :] == e, weights[1:2, :], 0.0)
        high = bf16(block * share)
        shares[0, e] = high
        shares[1, e] = bf16(block * share - f32(high))


N_MAIL = 30 + 15 + 2 * (4 + 6 + 40 + 48 + 12)


def shards(queries, keys, values, log_decay, doc_ids, residual, out_weight, norm_gain, expert_ids, route_weight, w_gate, w_up, w_down):
    vmem = pl.BlockSpec(memory_space=pltpu.VMEM)
    hbm = pl.BlockSpec(memory_space=pl.ANY)
    bf, fl = jnp.bfloat16, jnp.float32
    dma = pltpu.SemaphoreType.DMA
    unit = (2, CAP, HW)
    scratch = [
        ((T, HEADS * HS), bf), ((T, HEADS * HS), bf), ((T, HEADS * HS), bf), ((HEADS, T), fl), ((1, T), jnp.int32),
        ((1, SL * W), fl), ((2, T), jnp.int32), ((2, T), fl),
        ((SL, HEADS * HS, W), bf), ((T, W), bf), ((SL, CAP, T), bf), ((2, SL, CAP, T), bf),
        ((N_SEQ, 48, HS), bf), ((N_SEQ, 48, HS), bf), ((N_SEQ, 32, HS), bf), ((N_SEQ, 32, HS), bf),
        ((HEADS, T, HS), fl), ((HEADS, T, HS), bf), ((T, HEADS * HS), bf),
        ((2, 4, 2, HALF, HW), bf), ((2, 4, 2, HALF, HW), bf), ((2, 4, 2, HALF, HW), bf),
        ((2, 2, HALF, HW), bf), ((2, 2, 2, HALF, HW), bf),
        ((T, W), fl), ((2, SL, CAP, HW), bf), ((SL, CAP, 128), bf), ((SL, CAP, 128), bf), ((8, 128), fl), ((16, 8, 128), fl),
        ((16, SL) + unit, bf), ((16, SL) + unit, bf), ((2, 2 * F, 4 * W), bf), ((2, F, 4 * W), bf),
        ((4, 4 * CAP, 2 * F), fl), ((4, 4 * CAP, F), bf),
        ((2, 2, 4, 2) + unit, bf), ((2, 2, 4, 2, 2) + unit, bf), ((2, 2, 2) + unit, bf), ((2, 2, 2, 2) + unit, bf),
        ((SL,) + unit, bf), ((2, SL, CAP, HW), bf),
    ]
    return pl.pallas_call(
        layer_kernel,
        out_shape=jax.ShapeDtypeStruct((T, W), bf),
        in_specs=[hbm] * 13,
        out_specs=vmem,
        scratch_shapes=[pltpu.VMEM(*s) for s in scratch]
        + [dma((SL + SL + 1 + 6 * SL,)), dma((N_MAIL,)), dma((N_MAIL,)), dma((40,)), dma((40,))],
        compiler_params=pltpu.CompilerParams(collective_id=0, has_side_effects=True, vmem_limit_bytes=60 * 2**20),
        name="layer",
    )(queries, keys, values, log_decay.T, doc_ids.reshape(1, T), residual, out_weight, norm_gain.reshape(1, SL * W),
      expert_ids.T, route_weight.T, w_gate[0].T, w_up[0].T, w_down[0])


def solution(mesh):
    return jax.shard_map(
        shards,
        mesh=mesh,
        in_specs=(
            P("seq", "hx"),
            P("seq", "hx"),
            P("seq", "hx"),
            P("seq", "hx"),
            P("seq"),
            P("seq", None),
            P("hx", None),
            P(),
            P("seq", None),
            P("seq", None),
            P("hx", None, "seq"),
            P("hx", None, "seq"),
            P("hx", "seq", None),
        ),
        out_specs=P("seq", "hx"),
        check_vma=False,
    )
```
